32 devices in a mesh: lon: 16 (over z, y, core), lat: 2 (over x).
Axes of the slice: x: 2, y: 2, z: 4, core: 2. Of those that a mesh axis runs over, the one named last changes fastest.
Arguments:
- state: float32 [4, 32, 64, 2048], P(None, None, 'lat', 'lon'), may hold values from -6 to 6
- land_mask: int32 [64, 2048], P('lat', 'lon'), may hold values 0 or 1
- wet_levels: int32 [64, 2048], P('lat', 'lon'), may hold values from 1 to 32
Outputs:
- new_state: float32 [4, 32, 64, 2048], P(None, None, 'lat', 'lon')
The draws below stay inside these ranges and needn't reach their ends.
All inputs are finite; a program needn't handle non-finite values. No bound on the sum of `land_mask` on one device may be relied on, other than what follows from the above.
Results may differ from the reference program's by a relative error of at most 0.00002.
Values sent between devices are 32-bit elements; how exact they have to be, the bound alone decides.
No kernel may reach another device: no remote copies, remote signals or barrier semaphores. Data moves between devices by JAX's collectives and lax.ppermute only.
A program may use at most 128 MiB of HBM per device.

```python
import jax
import jax.numpy as jnp
from jax import lax

LEV = 32
STEPS = 2
NY = 64
NX = 2048


def set_ends(entries, stream_key, smallest, top_value):
    longest = entries.shape.index(max(entries.shape))
    spots = []
    for shift in (0, 1):
        where = [jax.random.randint(jax.random.fold_in(stream_key, axis), (), 0, length) for axis, length in enumerate(entries.shape)]
        where[longest] = (where[longest] + shift) % entries.shape[longest]
        spots.append(tuple(where))
    return entries.at[spots[0]].set(smallest).at[spots[1]].set(top_value)


def shard_levels(own_key, extent, shards, low, high):
    level, own = 1.0, jax.random.fold_in(own_key, 6)
    for axis_at, blocks in shards:
        draws = jnp.exp(jax.random.uniform(jax.random.fold_in(own, axis_at), (blocks,), jnp.float32, low / len(shards), high / len(shards)))
        level = level * jnp.repeat(draws, extent[axis_at] // blocks).reshape([-1 if axis == axis_at else 1 for axis in range(len(extent))])
    return level


def gaussian(rng, dims, scale, limit, shards=(), held_as=jnp.bfloat16):
    entries = jax.random.normal(rng, dims, jnp.float32) * scale
    if len(shards) > 0:
        entries = shard_levels(rng, dims, shards, -0.22, 0.18) * entries
    return jnp.clip(entries, min=-limit, max=limit).astype(held_as)


def setup_inputs(seed: int = 0) -> dict:
    seeds = jax.random.split(jax.random.key(seed), 4)
    state = gaussian(seeds[0], (4, LEV, NY, NX), 1.0, 6.0, ((2, 2), (3, 16)), jnp.float32)
    land_mask = set_ends((jax.random.randint(seeds[1], (NY, NX), 0, 4) < 3).astype(jnp.int32), jax.random.fold_in(seeds[1], 1), 0, 1)
    wet_levels = set_ends(jax.random.randint(seeds[2], (NY, NX), 1, LEV + 1), jax.random.fold_in(seeds[2], 1), 1, LEV).astype(jnp.int32)
    return dict(state=state, land_mask=land_mask, wet_levels=wet_levels)


time_step = 0.1
lateral_mix = 0.5
column_mix = 0.5
gravity = 0.5
thermal = 0.2
haline = 0.8


def wetness(land_mask, wet_levels, levels):
    level_ids = jnp.arange(levels, dtype=jnp.int32)[:, None, None]
    return ((land_mask[None] == 1) & (level_ids < wet_levels[None])).astype(jnp.float32)


def pressure(extended):
    density = haline * extended[1] - thermal * extended[0]
    return gravity * (jnp.cumsum(density, axis=0) - 0.5 * density)


def explicit(state, east_west, north_south, press_ew, press_ns, coriolis, wet):
    grad_x = (8.0 * (east_west[..., 3:-1] - east_west[..., 1:-3]) - (east_west[..., 4:] - east_west[..., :-4])) / 12.0
    grad_y = (8.0 * (north_south[..., 3:-1, :] - north_south[..., 1:-3, :]) - (north_south[..., 4:, :] - north_south[..., :-4, :])) / 12.0
    spread = (east_west[..., 3:-1] + east_west[..., 1:-3]) + (north_south[..., 3:-1, :] + north_south[..., 1:-3, :]) - 4.0 * state
    east_vel = state[2]
    north_vel = state[3]
    carried = east_vel * grad_x + north_vel * grad_y
    press_x = 0.5 * (press_ew[..., 3:-1] - press_ew[..., 1:-3])
    press_y = 0.5 * (press_ns[..., 3:-1, :] - press_ns[..., 1:-3, :])
    zero = jnp.zeros_like(press_x)
    force = jnp.stack([zero, zero, coriolis * north_vel - press_x, -coriolis * east_vel - press_y])
    return (state + time_step * (lateral_mix * spread - carried + force)) * wet


def reference(state, land_mask, wet_levels):
    levels = state.shape[1]
    rows = state.shape[2]
    cols = state.shape[3]
    wet = wetness(land_mask, wet_levels, levels)
    coriolis = (0.2 + 0.8 * ((jnp.arange(rows, dtype=jnp.int32).astype(jnp.float32) + 0.5) / rows))[:, None]
    sign = jnp.array([1.0, 1.0, -1.0, -1.0], jnp.float32)[:, None, None, None]
    upper = jnp.concatenate([column_mix * wet[1:], jnp.zeros_like(wet[:1])], axis=0)
    lower = jnp.concatenate([jnp.zeros_like(wet[:1]), column_mix * wet[1:]], axis=0)
    centre = 1.0 + lower + upper
    current = state * wet
    for step in range(STEPS):
        east_west = jnp.concatenate([current[..., -2:], current, current[..., :2]], axis=3)
        fold = sign * current[:, :, -2:, ::-1][:, :, ::-1, :]
        north_south = jnp.concatenate([jnp.zeros_like(current[:, :, :2]), current, fold], axis=2)
        press_ew = pressure(east_west)
        press_ns = pressure(north_south)

        def one_level(level):
            return explicit(current[:, level], east_west[:, level], north_south[:, level],
                            press_ew[level], press_ns[level], coriolis, wet[level])

        levels_first = lax.map(one_level, jnp.arange(levels, dtype=jnp.int32))

        def forward(carry, inputs):
            ratio_prev, part_prev = carry
            rhs, low, high, middle = inputs
            denom = middle + low * ratio_prev
            ratio = -high / denom
            part = (rhs + low * part_prev) / denom
            return (ratio, part), (ratio, part)

        start = (jnp.zeros((rows, cols), jnp.float32), jnp.zeros((4, rows, cols), jnp.float32))
        unused, (ratios, parts) = lax.scan(forward, start, (levels_first, lower, upper, centre))

        def backward(below, inputs):
            ratio, part = inputs
            value = part - ratio * below
            return value, value

        unused_last, values = lax.scan(backward, jnp.zeros((4, rows, cols), jnp.float32), (ratios, parts), reverse=True)
        current = jnp.moveaxis(values, 0, 1)
    return current
```

```python
import functools

import jax
import jax.numpy as jnp
import numpy as np
from jax import lax
from jax.experimental import pallas as pl
from jax.experimental.pallas import tpu as pltpu
from jax.sharding import PartitionSpec as P

STEPS = 2
time_step = 0.1
lateral_mix = 0.5
column_mix = 0.5
gravity = 0.5
thermal = 0.2
haline = 0.8

F32 = jnp.float32
VM = pl.BlockSpec(memory_space=pltpu.VMEM)
SM = pl.BlockSpec(memory_space=pltpu.SMEM)
HB = pl.BlockSpec(memory_space=pltpu.HBM)
PARAMS = pltpu.CompilerParams(vmem_limit_bytes=12 * 2**20)


def factors(levels):
    inner = np.zeros(levels)
    lowest = np.zeros(levels)
    for k in range(levels):
        over = column_mix if k > 0 else 0.0
        less = column_mix * column_mix * inner[k - 1] if k > 0 else 0.0
        inner[k] = 1.0 / (1.0 + over + column_mix - less)
        lowest[k] = 1.0 / (1.0 + over - less)
    return np.stack([inner, lowest, column_mix * inner]).astype(np.float32)


def lanes():
    return lax.broadcasted_iota(jnp.int32, (8, 128), 1)


def sublanes():
    return lax.broadcasted_iota(jnp.int32, (8, 128), 0)


def pack_kernel(place, state, land, wet, p1, p2, la, lb, main, depth, held, held_land, held_wet, sems):
    levels, rows = state.shape[1], state.shape[2]
    groups = rows // 8
    chunk = levels // 4
    copies = [
        pltpu.make_async_copy(land, held_land, sems.at[4]),
        pltpu.make_async_copy(wet, held_wet, sems.at[5]),
    ] + [
        pltpu.make_async_copy(state.at[:, c * chunk:(c + 1) * chunk], held.at[:, c * chunk:(c + 1) * chunk], sems.at[c])
        for c in range(4)
    ]
    for copy in copies:
        copy.start()
    copies[0].wait()
    copies[1].wait()
    lon_even = place[0] == 0
    band_even = place[1] == 0
    depth[0:8, :] = jnp.zeros((8, 128), F32)
    depth[rows:rows + 8, :] = jnp.zeros((8, 128), F32)
    deeps = []
    for g in range(groups):
        at = slice(8 * g, 8 * g + 8)
        deep = jnp.where(held_land[at, :] == 1, jnp.minimum(held_wet[at, :], levels), 0).astype(F32)
        depth[8 * g + 4:8 * g + 12, :] = deep
        deeps.append(deep)
    group = lanes() >> 2
    low = sublanes() < 4

    def edges(a0, a3, b0, b3):
        north = jnp.where(low, pltpu.roll(a3, 4, 0), b3)
        south = jnp.where(low, a0, pltpu.roll(b0, 4, 0))
        return jnp.where(band_even, north, south), jnp.where(band_even, south, north)

    def body(k, unused):
        level = k.astype(F32)
        spot_e = group == k
        spot_w = group == ((k + 1) & (levels - 1))
        for pair in range(2):
            tiles = []
            for f in (2 * pair, 2 * pair + 1):
                for g in range(groups):
                    at = slice(8 * g, 8 * g + 8)
                    q = jnp.where(level < deeps[g], held[f, k, at, :], 0.0)
                    main[f, k, 8 * g + 4:8 * g + 12, :] = q
                    tiles.append(q)
                    turned = pltpu.roll(q, (4 * k + 4) & 127, 1)
                    la[f, at, :] = jnp.where(spot_e, turned, la[f, at, :])
                    lb[f, at, :] = jnp.where(spot_w, turned, lb[f, at, :])
            first, second = edges(tiles[0], tiles[groups - 1], tiles[groups], tiles[2 * groups - 1])
            p1[2 * k + pair] = first
            p2[2 * k + pair] = second
        return unused

    for c in range(4):
        copies[2 + c].wait()
        lax.fori_loop(c * chunk, (c + 1) * chunk, body, 0, unroll=4)
    for g in range(groups):
        turned = pltpu.roll(deeps[g], 4, 1)
        la[4, 8 * g:8 * g + 8, :] = turned
        lb[4, 8 * g:8 * g + 8, :] = turned
    first, second = edges(deeps[0], deeps[-1], deeps[0], deeps[-1])
    p1[2 * levels] = first
    p2[2 * levels] = second

    @pl.when(jnp.logical_not(lon_even))
    def _():
        for f in range(5):
            for g in range(groups):
                at = slice(8 * g, 8 * g + 8)
                east, west = la[f, at, :], lb[f, at, :]
                la[f, at, :] = west
                lb[f, at, :] = east


def coriolis_rows(first, total):
    row = first + sublanes()
    row = jnp.where(row >= total, 2 * total - 1 - row, row)
    return 0.2 + 0.8 * ((row.astype(F32) + 0.5) / total.astype(F32))


def sweep(table, levels, jobs, unroll=8, unroll_back=8):
    lane = lanes()
    zero = jnp.zeros((8, 128), F32)

    def forward(k, carry):
        inner, lowest = table[0, k], table[1, k]
        level = k.astype(F32)
        out = []
        for n, (own, other, o, depth, cor, dst, d) in enumerate(jobs):
            parts = carry[6 * n:6 * n + 4]
            cum_x, cum_y = carry[6 * n + 4:6 * n + 6]
            weight = jnp.where(level < depth - 1.0, inner, jnp.where(level < depth, lowest, 0.0))
            q = [own[f, k, o:o + 8, :] for f in range(4)]
            cu = q[2] * (time_step / 12.0)
            cv = q[3] * (time_step / 12.0)
            prov = []
            near = []
            for f in range(4):
                x = other[f, k, o:o + 8, :]
                e1 = pltpu.roll(jnp.where(lane == 0, x, q[f]), 127, 1)
                e2 = pltpu.roll(jnp.where(lane < 2, x, q[f]), 126, 1)
                w1 = pltpu.roll(jnp.where(lane == 127, x, q[f]), 1, 1)
                w2 = pltpu.roll(jnp.where(lane >= 126, x, q[f]), 2, 1)
                n1 = own[f, k, o + 1:o + 9, :]
                n2 = own[f, k, o + 2:o + 10, :]
                s1 = own[f, k, o - 1:o + 7, :]
                s2 = own[f, k, o - 2:o + 6, :]
                dx, dy = e1 - w1, n1 - s1
                near.append((dx, dy))
                spread = (e1 + w1) + (n1 + s1)
                value = (1.0 - 4.0 * time_step * lateral_mix) * q[f] + (time_step * lateral_mix) * spread
                value = value - cu * (8.0 * dx - (e2 - w2)) - cv * (8.0 * dy - (n2 - s2))
                prov.append(value)
            dens_x = haline * near[1][0] - thermal * near[0][0]
            dens_y = haline * near[1][1] - thermal * near[0][1]
            cum_x = cum_x + dens_x
            cum_y = cum_y + dens_y
            press = time_step * gravity * 0.5
            prov[2] = prov[2] + (time_step * cor) * q[3] - press * (cum_x - 0.5 * dens_x)
            prov[3] = prov[3] - (time_step * cor) * q[2] - press * (cum_y - 0.5 * dens_y)
            for f in range(4):
                part = (prov[f] + column_mix * parts[f]) * weight
                dst[f, k, d:d + 8, :] = part
                out.append(part)
            out += [cum_x, cum_y]
        return tuple(out)

    lax.fori_loop(0, levels, forward, (zero,) * (6 * len(jobs)), unroll=unroll)

    def backward(step, carry):
        k = levels - 1 - step
        ratio = table[2, k]
        out = []
        for n, (own, other, o, depth, cor, dst, d) in enumerate(jobs):
            for f in range(4):
                value = dst[f, k, d:d + 8, :] + ratio * carry[4 * n + f]
                dst[f, k, d:d + 8, :] = value
                out.append(value)
        return tuple(out)

    lax.fori_loop(0, levels, backward, (zero,) * (4 * len(jobs)), unroll=unroll_back)


def side_tile(east, west, group, k):
    return pltpu.roll(jnp.where(group == k, west, east), (124 - 4 * k) & 127, 1)


def spread_corner(corner, shift):
    return pltpu.roll(corner, shift & 127, 1)


def inner_kernel(place, table, main0, depth, ra, rb, out, side0, side1, main1, side_depth, last, sem):
    levels, rows = main0.shape[1], out.shape[2]
    groups = rows // 8
    lon_even = place[0] == 0
    first_row, total = place[2], place[3]
    group = lanes() >> 2
    zero = jnp.zeros((8, 128), F32)

    def both(f, g):
        at = slice(8 * g, 8 * g + 8)
        a, b = ra[f, at, :], rb[f, at, :]
        return jnp.where(lon_even, a, b), jnp.where(lon_even, b, a)

    side_depth[0:8, :] = zero
    side_depth[rows:rows + 8, :] = zero
    for g in range(groups):
        east, west = both(4, g)
        side_depth[8 * g + 4:8 * g + 12, :] = side_tile(east, west, group, 0)
    for f in range(4):
        pairs = [both(f, g) for g in range(groups)]

        def fill(k, unused):
            for g in range(groups):
                side0[f, k, 8 * g + 4:8 * g + 12, :] = side_tile(*pairs[g], group, k)
            return unused

        lax.fori_loop(0, levels, fill, 0, unroll=4)

    jobs = []
    for w in range(1, groups):
        o = 8 * w + 2
        cor = coriolis_rows(first_row + (8 * w - 2), total)
        jobs.append((main0, side0, o, depth[o:o + 8, :], cor, main1, 8 * w))
        jobs.append((side0, main0, o, side_depth[o:o + 8, :], cor, side1, 8 * w))
    sweep(table, levels, jobs, 4, 4)
    jobs = []
    for w in range(1, groups - 1):
        cor = coriolis_rows(first_row + 8 * w, total)
        jobs.append((main1, side1, 8 * w + 2, depth[8 * w + 4:8 * w + 12, :], cor, last, 8 * w - 8))
    sweep(table, levels, jobs)
    copy = pltpu.make_async_copy(last, out.at[:, :, 8:rows - 8, :], sem)
    copy.start()
    copy.wait()


def south_kernel(place, table, p, corner, depth, side_depth, main0, side0, main1, side1, before, out,
                 rim0, edge0, rim1, edge1, last, sem):
    levels = main0.shape[1]
    first_row, total = place[2], place[3]
    has_south = first_row > 0
    edge = jnp.where(has_south, corner[...], 0.0)
    rim_depth = jnp.where(has_south, p[2 * levels], 0.0)
    depths = jnp.where(sublanes() < 2, pltpu.roll(rim_depth, 6, 0), depth[2:10, :])

    def fill(k, unused):
        corners = spread_corner(edge, 124 - 4 * k)
        for pair in range(2):
            rim = jnp.where(has_south, p[2 * k + pair], 0.0)
            for j in range(2):
                f = 2 * pair + j
                rim0[f, k, 0:4, :] = rim[4 * j:4 * j + 4, :]
                rim0[f, k, 4:12, :] = main0[f, k, 4:12, :]
                edge0[f, k, 0:2, :] = jnp.zeros((2, 128), F32)
                edge0[f, k, 2:4, :] = corners[2 * f:2 * f + 2, :]
                edge0[f, k, 4:12, :] = side0[f, k, 4:12, :]
                rim1[f, k, 8:12, :] = main1[f, k, 8:12, :]
                edge1[f, k, 8:12, :] = side1[f, k, 8:12, :]
        return unused

    lax.fori_loop(0, levels, fill, 0, unroll=4)
    cor = coriolis_rows(first_row - 2, total)
    sweep(table, levels, [
        (rim0, edge0, 2, depths, cor, rim1, 0),
        (edge0, rim0, 2, side_depth[2:10, :], cor, edge1, 0),
    ])
    cor = coriolis_rows(first_row, total)
    sweep(table, levels, [(rim1, edge1, 2, depth[4:12, :], cor, last, 0)])
    copy = pltpu.make_async_copy(last, out.at[:, :, 0:8, :], sem)
    copy.start()
    copy.wait()


def north_kernel(place, table, p1, p2, c1, c2, depth, side_depth, main0, side0, main1, side1, before, out,
                 rim0, edge0, rim1, edge1, last, sem):
    levels, rows = main0.shape[1], out.shape[2]
    band_even = place[1] == 0
    first_row, total = place[2], place[3]
    is_top = first_row + rows == total
    mirror = 127 - lanes()
    flip = sublanes() ^ 3

    def ghost(index, sign):
        far = p2[index]
        folded = jnp.take_along_axis(far, mirror, axis=1, mode="promise_in_bounds")
        folded = jnp.take_along_axis(folded, flip, axis=0, mode="promise_in_bounds") * sign
        return jnp.where(band_even, p1[index], jnp.where(is_top, folded, far))

    far = c2[...]
    folded = jnp.take_along_axis(far, mirror, axis=1, mode="promise_in_bounds")
    folded = jnp.where(sublanes() < 4, folded, -folded)
    corner = jnp.where(band_even, c1[...], jnp.where(is_top, folded, far))
    depths = jnp.where(sublanes() < 6, depth[rows - 2:rows + 6, :], pltpu.roll(ghost(2 * levels, 1.0), 6, 0))

    def fill(k, unused):
        corners = spread_corner(corner, jnp.where(is_top, 4 * k - 124, 124 - 4 * k))
        for pair in range(2):
            rim = ghost(2 * k + pair, 1.0 if pair == 0 else -1.0)
            for j in range(2):
                f = 2 * pair + j
                rim0[f, k, 0:8, :] = main0[f, k, rows - 4:rows + 4, :]
                rim0[f, k, 8:12, :] = rim[4 * j:4 * j + 4, :]
                edge0[f, k, 0:8, :] = side0[f, k, rows - 4:rows + 4, :]
                edge0[f, k, 8:10, :] = corners[2 * f:2 * f + 2, :]
                edge0[f, k, 10:12, :] = jnp.zeros((2, 128), F32)
                rim1[f, k, 0:4, :] = main1[f, k, rows - 8:rows - 4, :]
                edge1[f, k, 0:4, :] = side1[f, k, rows - 8:rows - 4, :]
        return unused

    lax.fori_loop(0, levels, fill, 0, unroll=4)
    cor = coriolis_rows(first_row + (rows - 6), total)
    sweep(table, levels, [
        (rim0, edge0, 2, depths, cor, rim1, 4),
        (edge0, rim0, 2, side_depth[rows - 2:rows + 6, :], cor, edge1, 4),
    ])
    cor = coriolis_rows(first_row + (rows - 8), total)
    sweep(table, levels, [(rim1, edge1, 2, depth[rows - 4:rows + 4, :], cor, last, 0)])
    copy = pltpu.make_async_copy(last, out.at[:, :, rows - 8:rows, :], sem)
    copy.start()
    copy.wait()


def per_device(state, land_mask, wet_levels):
    fields, levels, rows, cols = state.shape
    lon, lat = lax.axis_index("lon"), lax.axis_index("lat")
    count, bands = lax.axis_size("lon"), lax.axis_size("lat")
    place = jnp.stack([lon & 1, lat & 1, lat * rows, bands * rows]).astype(jnp.int32)
    table = jnp.asarray(factors(levels))

    def mate(i):
        return i ^ 1

    def beyond(i):
        return (i + 1) % count if i % 2 else (i - 1) % count

    def swap(x, to):
        pairs = []
        for i in range(count):
            for b in range(bands):
                ti, tb = to(i, b)
                pairs.append((i * bands + b, ti * bands + tb))
        return lax.ppermute(x, ("lon", "lat"), pairs)

    def near(i, b):
        return i, b ^ 1

    def far(i, b):
        if b == bands - 1:
            return count - 1 - i, b
        if b == 0:
            return i, b
        return i, (b + 1 if b % 2 else b - 1)

    call = functools.partial(pl.pallas_call, compiler_params=PARAMS)
    shape = lambda *dims: jax.ShapeDtypeStruct(dims, F32)
    block = lambda n: shape(fields, levels, n, 128)
    room = lambda n: pltpu.VMEM((fields, levels, n, 128), F32)
    edge, strip = shape(2 * levels + 1, 8, 128), shape(5, rows, 128)
    p1, p2, la, lb, main0, depth = call(
        pack_kernel,
        out_shape=(edge, edge, strip, strip, block(rows + 8), shape(rows + 8, 128)),
        in_specs=[SM, HB, HB, HB],
        out_specs=(VM,) * 6,
        scratch_shapes=[room(rows), pltpu.VMEM((rows, 128), jnp.int32), pltpu.VMEM((rows, 128), jnp.int32),
                        pltpu.SemaphoreType.DMA((6,))],
        name="pack",
    )(place, state, land_mask, wet_levels)
    rp2 = swap(p2, far)
    rb = swap(lb, lambda i, b: (beyond(i), b))
    ra = swap(la, lambda i, b: (mate(i), b))
    rp1 = swap(p1, near)

    lon_even = lon & 1 == 0
    band_even = lat & 1 == 0
    lane = jnp.arange(128, dtype=jnp.int32)
    ends = lambda x: (x[:4, 0:2], x[:4, rows - 2:rows])
    (a_low, a_high), (b_low, b_high) = ends(ra), ends(rb)
    from_east = (lane % 4 < 2) == lon_even
    low = jnp.where(from_east, a_low, b_low)
    high = jnp.where(from_east, a_high, b_high)
    back = jnp.where(lat == bands - 1, high[:, ::-1], high)
    rc1 = swap(jnp.where(band_even, high, low).reshape(8, 128), near)
    rc2 = swap(jnp.where(band_even, low, back).reshape(8, 128), far)

    if bands == 2:
        south, south_corner = rp1, rc1
    else:
        south = jnp.where(band_even, rp2, rp1)
        south_corner = jnp.where(band_even, rc2, rc1)

    out, side0, side1, main1, side_depth = call(
        inner_kernel,
        out_shape=(shape(*state.shape), block(rows + 8), block(rows + 4), block(rows + 4), shape(rows + 8, 128)),
        in_specs=[SM, SM] + [VM] * 4,
        out_specs=(HB, VM, VM, VM, VM),
        scratch_shapes=[room(rows - 16), pltpu.SemaphoreType.DMA],
        name="inner",
    )(place, table, main0, depth, ra, rb)
    rim = functools.partial(
        call,
        out_shape=shape(*state.shape),
        out_specs=HB,
        scratch_shapes=[room(16)] * 4 + [room(8), pltpu.SemaphoreType.DMA],
    )
    out = rim(
        south_kernel,
        in_specs=[SM, SM] + [VM] * 8 + [HB],
        input_output_aliases={10: 0},
        name="south",
    )(place, table, south, south_corner, depth, side_depth, main0, side0, main1, side1, out)
    return rim(
        north_kernel,
        in_specs=[SM, SM] + [VM] * 10 + [HB],
        input_output_aliases={12: 0},
        name="north",
    )(place, table, rp1, rp2, rc1, rc2, depth, side_depth, main0, side0, main1, side1, out)


def solution(mesh):
    placed = (P(None, None, "lat", "lon"), P("lat", "lon"), P("lat", "lon"))
    return jax.shard_map(
        per_device,
        mesh=mesh,
        in_specs=placed,
        out_specs=P(None, None, "lat", "lon"),
        check_vma=False,
    )
```

```python
import functools

import jax
import jax.numpy as jnp
import numpy as np
from jax import lax
from jax.experimental import pallas as pl
from jax.experimental.pallas import tpu as pltpu
from jax.sharding import PartitionSpec as P

STEPS = 2
time_step = 0.1
lateral_mix = 0.5
column_mix = 0.5
gravity = 0.5
thermal = 0.2
haline = 0.8

F32 = jnp.float32
VM = pl.BlockSpec(memory_space=pltpu.VMEM)
HB = pl.BlockSpec(memory_space=pltpu.HBM)


UNIT = 1.0 / (time_step * lateral_mix)
GAIN = column_mix * UNIT
CENTRE = UNIT * (1.0 - 4.0 * time_step * lateral_mix)
DRIFT = UNIT * time_step / 12.0
PRESS = UNIT * time_step * 0.5 * gravity * 0.5


def factors(levels):
    inner = np.zeros(levels)
    lowest = np.zeros(levels)
    for k in range(levels):
        over = column_mix if k > 0 else 0.0
        less = column_mix * inner[k - 1] if k > 0 else 0.0
        inner[k] = column_mix / (1.0 + over + column_mix - less)
        lowest[k] = column_mix / (1.0 + over - less)
    return np.stack([inner, lowest]).astype(np.float32)


def fill_table(table):
    for n, row in enumerate(factors(table.shape[1])):
        for k, value in enumerate(row):
            table[n, k] = float(value)


def lanes():
    return lax.broadcasted_iota(jnp.int32, (8, 128), 1)


def sublanes():
    return lax.broadcasted_iota(jnp.int32, (8, 128), 0)


def pack_kernel(state, depth, p1, p2, la, lb):
    levels, rows = state.shape[1], state.shape[2]
    groups = rows // 8
    lon_even = lax.axis_index("lon") % 2 == 0
    band_even = lax.axis_index("lat") % 2 == 0
    zero = jnp.zeros((8, 128), F32)
    deeps = [depth[8 * g + 4:8 * g + 12, :] for g in range(groups)]
    group = lanes() >> 2
    low = sublanes() < 4

    def edges(a0, a3, b0, b3):
        north = jnp.where(low, pltpu.roll(a3, 4, 0), b3)
        south = jnp.where(low, a0, pltpu.roll(b0, 4, 0))
        return jnp.where(band_even, north, south), jnp.where(band_even, south, north)

    for pair in range(2):
        def body(k, accs):
            level = k.astype(F32)
            spot_e = group == k
            spot_w = group == ((k + 1) & (levels - 1))
            tiles = []
            new = []
            for j in range(2):
                for g in range(groups):
                    q = jnp.where(level < deeps[g], state[2 * pair + j, k, 8 * g:8 * g + 8, :], 0.0)
                    tiles.append(q)
                    turned = pltpu.roll(q, (4 * k + 4) & 127, 1)
                    new.append(jnp.where(spot_e, turned, accs[len(new)]))
                    new.append(jnp.where(spot_w, turned, accs[len(new)]))
            first, second = edges(tiles[0], tiles[groups - 1], tiles[groups], tiles[2 * groups - 1])
            p1[2 * k + pair] = first
            p2[2 * k + pair] = second
            return tuple(new)

        accs = lax.fori_loop(0, levels, body, (zero,) * (4 * groups), unroll=8)
        for j in range(2):
            for g in range(groups):
                at = slice(8 * g, 8 * g + 8)
                east, west = accs[2 * (j * groups + g)], accs[2 * (j * groups + g) + 1]
                la[2 * pair + j, at, :] = jnp.where(lon_even, east, west)
                lb[2 * pair + j, at, :] = jnp.where(lon_even, west, east)
    for g in range(groups):
        turned = pltpu.roll(deeps[g], 4, 1)
        la[4, 8 * g:8 * g + 8, :] = turned
        lb[4, 8 * g:8 * g + 8, :] = turned
    first, second = edges(deeps[0], deeps[-1], deeps[0], deeps[-1])
    p1[2 * levels] = first
    p2[2 * levels] = second


def coriolis_rows(first, total):
    row = first + sublanes()
    row = jnp.where(row >= total, 2 * total - 1 - row, row)
    return 0.2 + 0.8 * ((row.astype(F32) + 0.5) / total)


def sweep(table, levels, jobs, scale, leave=1.0, unroll=8, unroll_back=8):
    lane = lanes()
    zero = jnp.zeros((8, 128), F32)
    turns = [cor * (UNIT * time_step * scale / DRIFT) for _, _, _, _, cor, _, _ in jobs]
    uppers = [depth - 1.0 for _, _, _, depth, _, _, _ in jobs]

    def forward(k, carry):
        inner, lowest = table[0, k], table[1, k]
        level = k.astype(F32)
        out = []
        for n, (own, other, o, depth, _, dst, d) in enumerate(jobs):
            halves = carry[6 * n:6 * n + 4]
            sums = carry[6 * n + 4:6 * n + 6]
            weight = jnp.where(level < uppers[n], inner, jnp.where(level < depth, lowest, 0.0))
            q = [own[f, k, o:o + 8, :] for f in range(4)]
            cu = q[2] * (DRIFT / scale)
            cv = q[3] * (DRIFT / scale)
            prov = []
            near = []
            for f in range(4):
                x = other[f, k, o:o + 8, :]
                e1 = pltpu.roll(jnp.where(lane == 0, x, q[f]), 127, 1)
                e2 = pltpu.roll(jnp.where(lane < 2, x, q[f]), 126, 1)
                w1 = pltpu.roll(jnp.where(lane == 127, x, q[f]), 1, 1)
                w2 = pltpu.roll(jnp.where(lane >= 126, x, q[f]), 2, 1)
                n1 = own[f, k, o + 1:o + 9, :]
                n2 = own[f, k, o + 2:o + 10, :]
                s1 = own[f, k, o - 1:o + 7, :]
                s2 = own[f, k, o - 2:o + 6, :]
                dx, dy = e1 - w1, n1 - s1
                near.append((dx, dy))
                slope_x = 8.0 * dx - (e2 - w2)
                slope_y = 8.0 * dy - (n2 - s2)
                if f == 2:
                    slope_y = slope_y - turns[n]
                if f == 3:
                    slope_x = slope_x + turns[n]
                value = CENTRE * q[f] + ((e1 + w1) + (n1 + s1))
                prov.append(value - cu * slope_x - cv * slope_y)
            for axis in range(2):
                half = (PRESS * haline) * near[1][axis] - (PRESS * thermal) * near[0][axis]
                press = sums[axis] + half
                prov[2 + axis] = prov[2 + axis] - press
                near.append(press + half)
            for f in range(4):
                part = (prov[f] + halves[f]) * weight
                dst[f, k, d:d + 8, :] = part
                out.append(part)
            out += near[4:6]
        return tuple(out)

    lax.fori_loop(0, levels, forward, (zero,) * (6 * len(jobs)), unroll=unroll)

    def backward(step, carry):
        k = levels - 1 - step
        ratio = table[0, k]
        out = []
        for n, (_, _, _, _, _, dst, d) in enumerate(jobs):
            for f in range(4):
                value = dst[f, k, d:d + 8, :] + ratio * carry[4 * n + f]
                dst[f, k, d:d + 8, :] = value * leave if leave != 1.0 else value
                out.append(value)
        return tuple(out)

    lax.fori_loop(0, levels, backward, (zero,) * (4 * len(jobs)), unroll=unroll_back)


def side_tile(east, west, group, k):
    return pltpu.roll(jnp.where(group == k, west, east), (124 - 4 * k) & 127, 1)


def spread_corner(corner, shift):
    return pltpu.roll(corner, shift & 127, 1)


def inner_kernel(state, depth, ra, rb, main0, side0, side1, main1, side_depth, last, easts, wests, table):
    levels, rows = state.shape[1], state.shape[2]
    groups = rows // 8
    lon_even = lax.axis_index("lon") % 2 == 0
    first_row = lax.axis_index("lat") * rows
    total = rows * lax.axis_size("lat")
    fill_table(table)
    group = lanes() >> 2
    zero = jnp.zeros((8, 128), F32)

    for f in range(5):
        for g in range(groups):
            at = slice(8 * g, 8 * g + 8)
            a, b = ra[f, at, :], rb[f, at, :]
            easts[f, at, :] = jnp.where(lon_even, a, b)
            wests[f, at, :] = jnp.where(lon_even, b, a)
    side_depth[0:8, :] = zero
    side_depth[rows:rows + 8, :] = zero
    for g in range(groups):
        at = slice(8 * g, 8 * g + 8)
        side_depth[8 * g + 4:8 * g + 12, :] = side_tile(easts[4, at, :], wests[4, at, :], group, 0)

    def fill(k, unused):
        level = k.astype(F32)
        for g in range(groups):
            at = slice(8 * g, 8 * g + 8)
            to = slice(8 * g + 4, 8 * g + 12)
            is_wet = level < depth[to, :]
            for f in range(4):
                main0[f, k, to, :] = jnp.where(is_wet, state[f, k, at, :], 0.0)
                side0[f, k, to, :] = side_tile(easts[f, at, :], wests[f, at, :], group, k)
        return unused

    lax.fori_loop(0, levels, fill, 0, unroll=8)

    jobs = []
    for w in range(1, groups):
        o = 8 * w + 2
        cor = coriolis_rows(first_row + (8 * w - 2), total)
        jobs.append((main0, side0, o, depth[o:o + 8, :], cor, main1, 8 * w))
        jobs.append((side0, main0, o, side_depth[o:o + 8, :], cor, side1, 8 * w))
    sweep(table, levels, jobs, 1.0, 1.0, 8, 4)
    jobs = []
    for w in range(1, groups - 1):
        cor = coriolis_rows(first_row + 8 * w, total)
        jobs.append((main1, side1, 8 * w + 2, depth[8 * w + 4:8 * w + 12, :], cor, last, 8 * w - 8))
    sweep(table, levels, jobs, GAIN, 1.0 / GAIN**2, 16, 8)


def south_kernel(ps, cs, main0, side0, south0, south0e):
    levels = main0.shape[1]
    has_south = lax.axis_index("lat") > 0
    corner = jnp.where(has_south, cs[...], 0.0)

    def fill(k, unused):
        edge = spread_corner(corner, 124 - 4 * k)
        for pair in range(2):
            south = jnp.where(has_south, ps[2 * k + pair], 0.0)
            for j in range(2):
                f = 2 * pair + j
                south0[f, k, 0:4, :] = south[4 * j:4 * j + 4, :]
                south0[f, k, 4:12, :] = main0[f, k, 4:12, :]
                south0e[f, k, 0:2, :] = jnp.zeros((2, 128), F32)
                south0e[f, k, 2:4, :] = edge[2 * f:2 * f + 2, :]
                south0e[f, k, 4:12, :] = side0[f, k, 4:12, :]
        return unused

    lax.fori_loop(0, levels, fill, 0, unroll=4)


def rim_kernel(ps, p1, p2, c1, c2, depth, side_depth, south0, south0e, main0, side0, main1, side1, last, out,
               south1, south1e, north0, north0e, north1, north1e, ends, table, sems):
    levels, rows = main0.shape[1], out.shape[2]
    done = pltpu.make_async_copy(last, out.at[:, :, 8:rows - 8, :], sems.at[0])
    done.start()
    band = lax.axis_index("lat")
    band_even = band % 2 == 0
    first_row = band * rows
    total = rows * lax.axis_size("lat")
    has_south = band > 0
    is_top = band == lax.axis_size("lat") - 1
    fill_table(table)
    mirror = 127 - lanes()
    flip = sublanes() ^ 3

    south_rim = jnp.where(has_south, ps[2 * levels], 0.0)
    south_depth = jnp.where(sublanes() < 2, pltpu.roll(south_rim, 6, 0), depth[2:10, :])

    def ghost(index, sign):
        far = p2[index]
        folded = jnp.take_along_axis(far, mirror, axis=1, mode="promise_in_bounds")
        folded = jnp.take_along_axis(folded, flip, axis=0, mode="promise_in_bounds") * sign
        return jnp.where(band_even, p1[index], jnp.where(is_top, folded, far))

    far = c2[...]
    folded = jnp.take_along_axis(far, mirror, axis=1, mode="promise_in_bounds")
    folded = jnp.where(sublanes() < 4, folded, -folded)
    north_corner = jnp.where(band_even, c1[...], jnp.where(is_top, folded, far))
    north_depth = jnp.where(sublanes() < 6, depth[rows - 2:rows + 6, :], pltpu.roll(ghost(2 * levels, 1.0), 6, 0))

    def fill(k, unused):
        north_edge = spread_corner(north_corner, jnp.where(is_top, 4 * k - 124, 124 - 4 * k))
        for pair in range(2):
            north = ghost(2 * k + pair, 1.0 if pair == 0 else -1.0)
            for j in range(2):
                f = 2 * pair + j
                south1[f, k, 8:12, :] = main1[f, k, 8:12, :]
                south1e[f, k, 8:12, :] = side1[f, k, 8:12, :]
                north0[f, k, 0:8, :] = main0[f, k, rows - 4:rows + 4, :]
                north0[f, k, 8:12, :] = north[4 * j:4 * j + 4, :]
                north0e[f, k, 0:8, :] = side0[f, k, rows - 4:rows + 4, :]
                north0e[f, k, 8:10, :] = north_edge[2 * f:2 * f + 2, :]
                north0e[f, k, 10:12, :] = jnp.zeros((2, 128), F32)
                north1[f, k, 0:4, :] = main1[f, k, rows - 8:rows - 4, :]
                north1e[f, k, 0:4, :] = side1[f, k, rows - 8:rows - 4, :]
        return unused

    lax.fori_loop(0, levels, fill, 0, unroll=4)
    low = coriolis_rows(first_row - 2, total)
    high = coriolis_rows(first_row + (rows - 6), total)
    sweep(table, levels, [
        (south0, south0e, 2, south_depth, low, south1, 0),
        (south0e, south0, 2, side_depth[2:10, :], low, south1e, 0),
        (north0, north0e, 2, north_depth, high, north1, 4),
        (north0e, north0, 2, side_depth[rows - 2:rows + 6, :], high, north1e, 4),
    ], 1.0, 1.0, 16, 8)
    low = coriolis_rows(first_row, total)
    high = coriolis_rows(first_row + (rows - 8), total)
    sweep(table, levels, [
        (south1, south1e, 2, depth[4:12, :], low, ends, 0),
        (north1, north1e, 2, depth[rows - 4:rows + 4, :], high, ends, 8),
    ], GAIN, 1.0 / GAIN**2, 16, 8)
    first = pltpu.make_async_copy(ends.at[:, :, 0:8, :], out.at[:, :, 0:8, :], sems.at[1])
    second = pltpu.make_async_copy(ends.at[:, :, 8:16, :], out.at[:, :, rows - 8:rows, :], sems.at[2])
    first.start()
    second.start()
    done.wait()
    first.wait()
    second.wait()


def per_device(state, land_mask, wet_levels):
    fields, levels, rows, cols = state.shape
    lon, lat = lax.axis_index("lon"), lax.axis_index("lat")
    count, bands = lax.axis_size("lon"), lax.axis_size("lat")

    def mate(i):
        return i ^ 1

    def beyond(i):
        return (i + 1) % count if i % 2 else (i - 1) % count

    def swap(x, to):
        pairs = []
        for i in range(count):
            for b in range(bands):
                ti, tb = to(i, b)
                pairs.append((i * bands + b, ti * bands + tb))
        return lax.ppermute(x, ("lon", "lat"), pairs)

    def near(i, b):
        return i, b ^ 1

    def far(i, b):
        if b == bands - 1:
            return count - 1 - i, b
        if b == 0:
            return i, b
        return i, (b + 1 if b % 2 else b - 1)

    def call(kernel, vmem, **given):
        return pl.pallas_call(kernel, compiler_params=pltpu.CompilerParams(vmem_limit_bytes=vmem * 2**20), **given)

    shape = lambda *dims: jax.ShapeDtypeStruct(dims, F32)
    block = lambda n: shape(fields, levels, n, 128)
    room = lambda n: pltpu.VMEM((fields, levels, n, 128), F32)
    edge, strip = shape(2 * levels + 1, 8, 128), shape(5, rows, 128)
    depth = jnp.where(land_mask == 1, jnp.minimum(wet_levels, levels), 0).astype(F32)
    depth = jnp.pad(depth, ((4, 4), (0, 0)))
    p1, p2, la, lb = call(
        pack_kernel,
        6,
        out_shape=(edge, edge, strip, strip),
        in_specs=[VM] * 2,
        out_specs=(VM,) * 4,
        name="pack",
    )(state, depth)
    rp2 = swap(p2, far)
    rb = swap(lb, lambda i, b: (beyond(i), b))
    ra = swap(la, lambda i, b: (mate(i), b))
    rp1 = swap(p1, near)

    lon_even = lon & 1 == 0
    band_even = lat & 1 == 0
    lane = jnp.arange(128, dtype=jnp.int32)
    ends = lambda x: (x[:4, 0:2], x[:4, rows - 2:rows])
    (a_low, a_high), (b_low, b_high) = ends(ra), ends(rb)
    from_east = (lane % 4 < 2) == lon_even
    low = jnp.where(from_east, a_low, b_low)
    high = jnp.where(from_east, a_high, b_high)
    back = jnp.where(lat == bands - 1, high[:, ::-1], high)
    rc1 = swap(jnp.where(band_even, high, low).reshape(8, 128), near)
    rc2 = swap(jnp.where(band_even, low, back).reshape(8, 128), far)

    if bands == 2:
        south, south_corner = rp1, rc1
    else:
        south = jnp.where(band_even, rp2, rp1)
        south_corner = jnp.where(band_even, rc2, rc1)

    room_table = pltpu.SMEM((2, levels), F32)
    main0, side0, side1, main1, side_depth, last = call(
        inner_kernel,
        6,
        out_shape=(block(rows + 8), block(rows + 8), block(rows + 4), block(rows + 4), shape(rows + 8, 128),
                   block(rows - 16)),
        in_specs=[VM] * 4,
        out_specs=(VM,) * 6,
        scratch_shapes=[pltpu.VMEM((5, rows, 128), F32), pltpu.VMEM((5, rows, 128), F32), room_table],
        name="inner",
    )(state, depth, ra, rb)
    south0, south0e = call(
        south_kernel,
        4,
        out_shape=(block(16), block(16)),
        in_specs=[VM] * 4,
        out_specs=(VM,) * 2,
        name="south",
    )(south, south_corner, main0, side0)
    return call(
        rim_kernel,
        14,
        out_shape=shape(*state.shape),
        in_specs=[VM] * 14,
        out_specs=HB,
        scratch_shapes=[room(16)] * 7 + [room_table, pltpu.SemaphoreType.DMA((3,))],
        name="rim",
    )(south, rp1, rp2, rc1, rc2, depth, side_depth, south0, south0e, main0, side0, main1, side1, last)


def solution(mesh):
    placed = (P(None, None, "lat", "lon"), P("lat", "lon"), P("lat", "lon"))
    return jax.shard_map(
        per_device,
        mesh=mesh,
        in_specs=placed,
        out_specs=P(None, None, "lat", "lon"),
        check_vma=False,
    )
```

```python
import functools

import jax
import jax.numpy as jnp
import numpy as np
from jax import lax
from jax.experimental import pallas as pl
from jax.experimental.pallas import tpu as pltpu
from jax.sharding import PartitionSpec as P

STEPS = 2
time_step = 0.1
lateral_mix = 0.5
column_mix = 0.5
gravity = 0.5
thermal = 0.2
haline = 0.8

F32 = jnp.float32
VM = pl.BlockSpec(memory_space=pltpu.VMEM)
HB = pl.BlockSpec(memory_space=pltpu.HBM)


UNIT = 1.0 / (time_step * lateral_mix)
GAIN = column_mix * UNIT
CENTRE = UNIT * (1.0 - 4.0 * time_step * lateral_mix)
DRIFT = UNIT * time_step / 12.0
PRESS = UNIT * time_step * 0.5 * gravity * 0.5


def factors(levels):
    inner = np.zeros(levels)
    lowest = np.zeros(levels)
    for k in range(levels):
        over = column_mix if k > 0 else 0.0
        less = column_mix * inner[k - 1] if k > 0 else 0.0
        inner[k] = column_mix / (1.0 + over + column_mix - less)
        lowest[k] = column_mix / (1.0 + over - less)
    return np.stack([inner, lowest]).astype(np.float32)


def fill_table(table):
    for n, row in enumerate(factors(table.shape[1])):
        for k, value in enumerate(row):
            table[n, k] = float(value)


def lanes():
    return lax.broadcasted_iota(jnp.int32, (8, 128), 1)


def sublanes():
    return lax.broadcasted_iota(jnp.int32, (8, 128), 0)


def edge_rows(strip, f, r):
    rows = strip.shape[1]
    band = lax.axis_index("lat")
    band_even = band % 2 == 0
    is_top = band == lax.axis_size("lat") - 1
    south, north = strip[f, r:r + 1, :], strip[f, rows - 2 + r:rows - 1 + r, :]
    folded = strip[f, rows - 1 - r:rows - r, :]
    return jnp.where(band_even, north, south), jnp.where(band_even, south, jnp.where(is_top, folded, north))


def row_tiles(state, k, deep_s, deep_n, pair):
    rows = state.shape[2]
    level = k.astype(F32)
    tiles = []
    for f in (2 * pair, 2 * pair + 1):
        tiles.append(jnp.where(level < deep_s, state[f, k, 0:8, :], 0.0))
        tiles.append(jnp.where(level < deep_n, state[f, k, rows - 8:rows, :], 0.0))
    return join_rows(*tiles)


def join_rows(a_s, a_n, b_s, b_n):
    band_even = lax.axis_index("lat") % 2 == 0
    low = sublanes() < 4
    north = jnp.where(low, pltpu.roll(a_n, 4, 0), b_n)
    south = jnp.where(low, a_s, pltpu.roll(b_s, 4, 0))
    return jnp.where(band_even, north, south), jnp.where(band_even, south, north)


def far_kernel(state, depth, ra, p2):
    levels, rows = state.shape[1], state.shape[2]
    deep_s, deep_n = depth[4:12, :], depth[rows - 4:rows + 4, :]

    def body(k, unused):
        for pair in range(2):
            p2[2 * k + pair] = row_tiles(state, k, deep_s, deep_n, pair)[1]
        return unused

    lax.fori_loop(0, levels, body, 0, unroll=8)
    p2[2 * levels] = join_rows(deep_s, deep_n, deep_s, deep_n)[1]
    for f in range(4):
        for r in range(2):
            p2[2 * levels + 1, 2 * f + r:2 * f + r + 1, :] = edge_rows(ra, f, r)[1]
    for n in range(2 * levels + 2, p2.shape[0]):
        p2[n] = jnp.zeros((8, 128), F32)


def near_kernel(state, depth, ra, rb, p1):
    levels, rows = state.shape[1], state.shape[2]
    deep_s, deep_n = depth[4:12, :], depth[rows - 4:rows + 4, :]
    from_a = ((lanes()[0:1] & 3) < 2) == (lax.axis_index("lon") % 2 == 0)

    def body(k, unused):
        for pair in range(2):
            p1[2 * k + pair] = row_tiles(state, k, deep_s, deep_n, pair)[0]
        return unused

    lax.fori_loop(0, levels, body, 0, unroll=8)
    p1[2 * levels] = join_rows(deep_s, deep_n, deep_s, deep_n)[0]
    for f in range(4):
        for r in range(2):
            row = jnp.where(from_a, edge_rows(ra, f, r)[0], edge_rows(rb, f, r)[0])
            p1[2 * levels + 1, 2 * f + r:2 * f + r + 1, :] = row


def columns_kernel(state, depth, la, lb, cb):
    levels, rows = state.shape[1], state.shape[2]
    groups = rows // 8
    lon_even = lax.axis_index("lon") % 2 == 0
    zero = jnp.zeros((8, 128), F32)
    deeps = [depth[8 * g + 4:8 * g + 12, :] for g in range(groups)]
    group = lanes() >> 2
    for pair in range(2):
        def body(k, accs):
            level = k.astype(F32)
            spot_e = group == k
            spot_w = group == ((k + 1) & (levels - 1))
            new = []
            for j in range(2):
                for g in range(groups):
                    q = jnp.where(level < deeps[g], state[2 * pair + j, k, 8 * g:8 * g + 8, :], 0.0)
                    turned = pltpu.roll(q, (4 * k + 4) & 127, 1)
                    new.append(jnp.where(spot_e, turned, accs[len(new)]))
                    new.append(jnp.where(spot_w, turned, accs[len(new)]))
            return tuple(new)

        accs = lax.fori_loop(0, levels, body, (zero,) * (4 * groups), unroll=16)
        for j in range(2):
            for g in range(groups):
                at = slice(8 * g, 8 * g + 8)
                east, west = accs[2 * (j * groups + g)], accs[2 * (j * groups + g) + 1]
                la[2 * pair + j, at, :] = jnp.where(lon_even, east, west)
                lb[2 * pair + j, at, :] = jnp.where(lon_even, west, east)
    for g in range(groups):
        turned = pltpu.roll(deeps[g], 4, 1)
        la[4, 8 * g:8 * g + 8, :] = turned
        lb[4, 8 * g:8 * g + 8, :] = turned
    for f in range(4):
        for r in range(2):
            cb[2 * f + r:2 * f + r + 1, :] = edge_rows(lb, f, r)[1]


def coriolis_rows(first, total):
    row = first + sublanes()
    row = jnp.where(row >= total, 2 * total - 1 - row, row)
    return 0.2 + 0.8 * ((row.astype(F32) + 0.5) / total)


def sweep(table, levels, jobs, scale, leave=1.0, unroll=8, unroll_back=8):
    lane = lanes()
    zero = jnp.zeros((8, 128), F32)
    turns = [cor * (UNIT * time_step * scale / DRIFT) for _, _, _, _, cor, _, _ in jobs]
    uppers = [depth - 1.0 for _, _, _, depth, _, _, _ in jobs]

    def forward(k, carry):
        inner, lowest = table[0, k], table[1, k]
        level = k.astype(F32)
        out = []
        for n, (own, other, o, depth, _, dst, d) in enumerate(jobs):
            halves = carry[6 * n:6 * n + 4]
            sums = carry[6 * n + 4:6 * n + 6]
            weight = jnp.where(level < uppers[n], inner, jnp.where(level < depth, lowest, 0.0))
            q = [own[f, k, o:o + 8, :] for f in range(4)]
            cu = q[2] * (DRIFT / scale)
            cv = q[3] * (DRIFT / scale)
            prov = []
            near = []
            for f in range(4):
                x = other[f, k, o:o + 8, :]
                e1 = pltpu.roll(jnp.where(lane == 0, x, q[f]), 127, 1)
                e2 = pltpu.roll(jnp.where(lane < 2, x, q[f]), 126, 1)
                w1 = pltpu.roll(jnp.where(lane == 127, x, q[f]), 1, 1)
                w2 = pltpu.roll(jnp.where(lane >= 126, x, q[f]), 2, 1)
                n1 = own[f, k, o + 1:o + 9, :]
                n2 = own[f, k, o + 2:o + 10, :]
                s1 = own[f, k, o - 1:o + 7, :]
                s2 = own[f, k, o - 2:o + 6, :]
                dx, dy = e1 - w1, n1 - s1
                near.append((dx, dy))
                slope_x = 8.0 * dx - (e2 - w2)
                slope_y = 8.0 * dy - (n2 - s2)
                if f == 2:
                    slope_y = slope_y - turns[n]
                if f == 3:
                    slope_x = slope_x + turns[n]
                value = CENTRE * q[f] + ((e1 + w1) + (n1 + s1))
                prov.append(value - cu * slope_x - cv * slope_y)
            for axis in range(2):
                half = (PRESS * haline) * near[1][axis] - (PRESS * thermal) * near[0][axis]
                press = sums[axis] + half
                prov[2 + axis] = prov[2 + axis] - press
                near.append(press + half)
            for f in range(4):
                part = (prov[f] + halves[f]) * weight
                dst[f, k, d:d + 8, :] = part
                out.append(part)
            out += near[4:6]
        return tuple(out)

    lax.fori_loop(0, levels, forward, (zero,) * (6 * len(jobs)), unroll=unroll)

    def backward(step, carry):
        k = levels - 1 - step
        ratio = table[0, k]
        out = []
        for n, (_, _, _, _, _, dst, d) in enumerate(jobs):
            for f in range(4):
                value = dst[f, k, d:d + 8, :] + ratio * carry[4 * n + f]
                dst[f, k, d:d + 8, :] = value * leave if leave != 1.0 else value
                out.append(value)
        return tuple(out)

    lax.fori_loop(0, levels, backward, (zero,) * (4 * len(jobs)), unroll=unroll_back)


def side_tile(east, west, group, k):
    return pltpu.roll(jnp.where(group == k, west, east), (124 - 4 * k) & 127, 1)


def inner_kernel(state, depth, ra, rb, main0, side0, side1, main1, side_depth, last, easts, wests, table):
    levels, rows = state.shape[1], state.shape[2]
    groups = rows // 8
    lon_even = lax.axis_index("lon") % 2 == 0
    first_row = lax.axis_index("lat") * rows
    total = rows * lax.axis_size("lat")
    fill_table(table)
    group = lanes() >> 2
    zero = jnp.zeros((8, 128), F32)

    for f in range(5):
        for g in range(groups):
            at = slice(8 * g, 8 * g + 8)
            a, b = ra[f, at, :], rb[f, at, :]
            easts[f, at, :] = jnp.where(lon_even, a, b)
            wests[f, at, :] = jnp.where(lon_even, b, a)
    side_depth[0:8, :] = zero
    side_depth[rows:rows + 8, :] = zero
    for g in range(groups):
        at = slice(8 * g, 8 * g + 8)
        side_depth[8 * g + 4:8 * g + 12, :] = side_tile(easts[4, at, :], wests[4, at, :], group, 0)

    def fill(k, unused):
        level = k.astype(F32)
        for g in range(groups):
            at = slice(8 * g, 8 * g + 8)
            to = slice(8 * g + 4, 8 * g + 12)
            is_wet = level < depth[to, :]
            for f in range(4):
                main0[f, k, to, :] = jnp.where(is_wet, state[f, k, at, :], 0.0)
                side0[f, k, to, :] = side_tile(easts[f, at, :], wests[f, at, :], group, k)
        return unused

    lax.fori_loop(0, levels, fill, 0, unroll=16)

    jobs = []
    for w in range(1, groups):
        o = 8 * w + 2
        cor = coriolis_rows(first_row + (8 * w - 2), total)
        jobs.append((main0, side0, o, depth[o:o + 8, :], cor, main1, 8 * w))
        jobs.append((side0, main0, o, side_depth[o:o + 8, :], cor, side1, 8 * w))
    sweep(table, levels, jobs, 1.0, 1.0, 16, 8)
    jobs = []
    for w in range(1, groups - 1):
        cor = coriolis_rows(first_row + 8 * w, total)
        jobs.append((main1, side1, 8 * w + 2, depth[8 * w + 4:8 * w + 12, :], cor, last, 8 * w - 8))
    sweep(table, levels, jobs, GAIN, 1.0 / GAIN**2, 16, 8)


def south_kernel(p, depth, side_depth, main0, side0, main1, side1, last, rim0, edge0, rim1, edge1, table):
    levels = main0.shape[1]
    rows = depth.shape[0] - 8
    first_row = lax.axis_index("lat") * rows
    total = rows * lax.axis_size("lat")
    has_south = lax.axis_index("lat") > 0
    fill_table(table)
    corner = jnp.where(has_south, p[2 * levels + 1], 0.0)
    rim_depth = jnp.where(has_south, p[2 * levels], 0.0)
    depths = jnp.where(sublanes() < 2, pltpu.roll(rim_depth, 6, 0), depth[2:10, :])

    def fill(k, unused):
        corners = pltpu.roll(corner, (124 - 4 * k) & 127, 1)
        for pair in range(2):
            rim = jnp.where(has_south, p[2 * k + pair], 0.0)
            for j in range(2):
                f = 2 * pair + j
                rim0[f, k, 0:4, :] = rim[4 * j:4 * j + 4, :]
                rim0[f, k, 4:12, :] = main0[f, k, 4:12, :]
                edge0[f, k, 0:2, :] = jnp.zeros((2, 128), F32)
                edge0[f, k, 2:4, :] = corners[2 * f:2 * f + 2, :]
                edge0[f, k, 4:12, :] = side0[f, k, 4:12, :]
                rim1[f, k, 8:12, :] = main1[f, k, 8:12, :]
                edge1[f, k, 8:12, :] = side1[f, k, 8:12, :]
        return unused

    lax.fori_loop(0, levels, fill, 0, unroll=8)
    cor = coriolis_rows(first_row - 2, total)
    sweep(table, levels, [
        (rim0, edge0, 2, depths, cor, rim1, 0),
        (edge0, rim0, 2, side_depth[2:10, :], cor, edge1, 0),
    ], 1.0, 1.0, 16, 8)
    cor = coriolis_rows(first_row, total)
    sweep(table, levels, [(rim1, edge1, 2, depth[4:12, :], cor, last, 0)], GAIN, 1.0 / GAIN**2, 16, 8)


def north_kernel(p1, p2, cb, depth, side_depth, main0, side0, main1, side1, middle, south, out,
                 rim0, edge0, rim1, edge1, last, table, sems):
    levels, rows = main0.shape[1], out.shape[2]
    done = [
        pltpu.make_async_copy(middle, out.at[:, :, 8:rows - 8, :], sems.at[0]),
        pltpu.make_async_copy(south, out.at[:, :, 0:8, :], sems.at[1]),
    ]
    for copy in done:
        copy.start()
    band = lax.axis_index("lat")
    band_even = band % 2 == 0
    first_row = band * rows
    total = rows * lax.axis_size("lat")
    is_top = band == lax.axis_size("lat") - 1
    fill_table(table)
    mirror = 127 - lanes()
    flip = sublanes() ^ 3

    def folded(tile):
        return jnp.take_along_axis(tile, mirror, axis=1, mode="promise_in_bounds")

    def ghost(index, sign):
        far = p2[index]
        turned = jnp.take_along_axis(folded(far), flip, axis=0, mode="promise_in_bounds") * sign
        return jnp.where(band_even, p1[index], jnp.where(is_top, turned, far))

    sender_even = (lax.axis_index("lon") % 2 == 0) != is_top
    far = jnp.where(((lanes() & 3) < 2) == sender_even, p2[2 * levels + 1], cb[...])
    turned = jnp.where(sublanes() < 4, folded(far), -folded(far))
    corner = jnp.where(band_even, p1[2 * levels + 1], jnp.where(is_top, turned, far))
    depths = jnp.where(sublanes() < 6, depth[rows - 2:rows + 6, :], pltpu.roll(ghost(2 * levels, 1.0), 6, 0))

    def fill(k, unused):
        corners = pltpu.roll(corner, jnp.where(is_top, 4 * k - 124, 124 - 4 * k) & 127, 1)
        for pair in range(2):
            rim = ghost(2 * k + pair, 1.0 if pair == 0 else -1.0)
            for j in range(2):
                f = 2 * pair + j
                rim0[f, k, 0:8, :] = main0[f, k, rows - 4:rows + 4, :]
                rim0[f, k, 8:12, :] = rim[4 * j:4 * j + 4, :]
                edge0[f, k, 0:8, :] = side0[f, k, rows - 4:rows + 4, :]
                edge0[f, k, 8:10, :] = corners[2 * f:2 * f + 2, :]
                edge0[f, k, 10:12, :] = jnp.zeros((2, 128), F32)
                rim1[f, k, 0:4, :] = main1[f, k, rows - 8:rows - 4, :]
                edge1[f, k, 0:4, :] = side1[f, k, rows - 8:rows - 4, :]
        return unused

    lax.fori_loop(0, levels, fill, 0, unroll=8)
    cor = coriolis_rows(first_row + (rows - 6), total)
    sweep(table, levels, [
        (rim0, edge0, 2, depths, cor, rim1, 4),
        (edge0, rim0, 2, side_depth[rows - 2:rows + 6, :], cor, edge1, 4),
    ], 1.0, 1.0, 16, 8)
    cor = coriolis_rows(first_row + (rows - 8), total)
    sweep(table, levels, [(rim1, edge1, 2, depth[rows - 4:rows + 4, :], cor, last, 0)], GAIN, 1.0 / GAIN**2, 16, 8)
    copy = pltpu.make_async_copy(last, out.at[:, :, rows - 8:rows, :], sems.at[2])
    copy.start()
    for other in done:
        other.wait()
    copy.wait()


def per_device(state, land_mask, wet_levels):
    fields, levels, rows, cols = state.shape
    lon, lat = lax.axis_index("lon"), lax.axis_index("lat")
    count, bands = lax.axis_size("lon"), lax.axis_size("lat")

    def mate(i):
        return i ^ 1

    def beyond(i):
        return (i + 1) % count if i % 2 else (i - 1) % count

    def swap(x, to):
        pairs = []
        for i in range(count):
            for b in range(bands):
                ti, tb = to(i, b)
                pairs.append((i * bands + b, ti * bands + tb))
        return lax.ppermute(x, ("lon", "lat"), pairs)

    def near(i, b):
        return i, b ^ 1

    def far(i, b):
        if b == bands - 1:
            return count - 1 - i, b
        if b == 0:
            return i, b
        return i, (b + 1 if b % 2 else b - 1)

    def call(kernel, vmem, **given):
        return pl.pallas_call(kernel, compiler_params=pltpu.CompilerParams(vmem_limit_bytes=vmem * 2**20), **given)

    shape = lambda *dims: jax.ShapeDtypeStruct(dims, F32)
    block = lambda n: shape(fields, levels, n, 128)
    room = lambda n: pltpu.VMEM((fields, levels, n, 128), F32)
    strip = shape(5, rows, 128)
    depth = jnp.where(land_mask == 1, jnp.minimum(wet_levels, levels), 0).astype(F32)
    depth = jnp.pad(depth, ((4, 4), (0, 0)))
    la, lb, cb = call(
        columns_kernel, 4, out_shape=(strip, strip, shape(8, 128)), in_specs=[VM] * 2, out_specs=(VM,) * 3,
        name="columns",
    )(state, depth)
    ra = swap(la, lambda i, b: (mate(i), b))
    rb = swap(lb, lambda i, b: (beyond(i), b))
    rcb = swap(cb, lambda i, b: far(i if b == 0 else beyond(i), b))
    p2 = call(
        far_kernel, 4, out_shape=shape(2 * levels + 4, 8, 128), in_specs=[VM] * 3, out_specs=VM, name="far",
    )(state, depth, ra)
    rp2 = swap(p2, far)
    p1 = call(
        near_kernel, 4, out_shape=shape(2 * levels + 2, 8, 128), in_specs=[VM] * 4, out_specs=VM, name="near",
    )(state, depth, ra, rb)
    rp1 = swap(p1, near)
    south = rp1
    if bands > 2:
        same = jnp.where((jnp.arange(128) % 4 < 2) == (lon % 2 == 0), rp2[2 * levels + 1], rcb)
        south = jnp.where(lat % 2 == 0, rp2[:2 * levels + 2].at[2 * levels + 1].set(same), rp1)

    room_table = pltpu.SMEM((2, levels), F32)
    main0, side0, side1, main1, side_depth, last = call(
        inner_kernel,
        6,
        out_shape=(block(rows + 8), block(rows + 8), block(rows + 4), block(rows + 4), shape(rows + 8, 128),
                   block(rows - 16)),
        in_specs=[VM] * 4,
        out_specs=(VM,) * 6,
        scratch_shapes=[pltpu.VMEM((5, rows, 128), F32), pltpu.VMEM((5, rows, 128), F32), room_table],
        name="inner",
    )(state, depth, ra, rb)
    first = call(
        south_kernel,
        10,
        out_shape=block(8),
        in_specs=[VM] * 7,
        out_specs=VM,
        scratch_shapes=[room(16)] * 4 + [room_table],
        name="south",
    )(south, depth, side_depth, main0, side0, main1, side1)
    return call(
        north_kernel,
        12,
        out_shape=shape(*state.shape),
        in_specs=[VM] * 11,
        out_specs=HB,
        scratch_shapes=[room(16)] * 4 + [room(8), room_table, pltpu.SemaphoreType.DMA((3,))],
        name="north",
    )(rp1, rp2, rcb, depth, side_depth, main0, side0, main1, side1, last, first)


def solution(mesh):
    placed = (P(None, None, "lat", "lon"), P("lat", "lon"), P("lat", "lon"))
    return jax.shard_map(
        per_device,
        mesh=mesh,
        in_specs=placed,
        out_specs=P(None, None, "lat", "lon"),
        check_vma=False,
    )
```

```python
import functools

import jax
import jax.numpy as jnp
import numpy as np
from jax import lax
from jax.experimental import pallas as pl
from jax.experimental.pallas import tpu as pltpu
from jax.sharding import PartitionSpec as P

STEPS = 2
time_step = 0.1
lateral_mix = 0.5
column_mix = 0.5
gravity = 0.5
thermal = 0.2
haline = 0.8

F32 = jnp.float32
VM = pl.BlockSpec(memory_space=pltpu.VMEM)
HB = pl.BlockSpec(memory_space=pltpu.HBM)


UNIT = 1.0 / (time_step * lateral_mix)
GAIN = column_mix * UNIT
CENTRE = UNIT * (1.0 - 4.0 * time_step * lateral_mix)
DRIFT = UNIT * time_step / 12.0
PRESS = UNIT * time_step * 0.5 * gravity * 0.5


def factors(levels):
    inner = np.zeros(levels)
    lowest = np.zeros(levels)
    for k in range(levels):
        over = column_mix if k > 0 else 0.0
        less = column_mix * inner[k - 1] if k > 0 else 0.0
        inner[k] = column_mix / (1.0 + over + column_mix - less)
        lowest[k] = column_mix / (1.0 + over - less)
    return np.stack([inner, lowest]).astype(np.float32)


def fill_table(table):
    for n, row in enumerate(factors(table.shape[1])):
        for k, value in enumerate(row):
            table[n, k] = float(value)


def lanes():
    return lax.broadcasted_iota(jnp.int32, (8, 128), 1)


def sublanes():
    return lax.broadcasted_iota(jnp.int32, (8, 128), 0)


def limit_kernel(levels, top):
    top[...] = jnp.full(top.shape, float(levels), F32)


def edge_rows(strip, f, r):
    rows = strip.shape[1]
    band = lax.axis_index("lat")
    band_even = band % 2 == 0
    is_top = band == lax.axis_size("lat") - 1
    south, north = strip[f, r:r + 1, :], strip[f, rows - 2 + r:rows - 1 + r, :]
    folded = strip[f, rows - 1 - r:rows - r, :]
    return jnp.where(band_even, north, south), jnp.where(band_even, south, jnp.where(is_top, folded, north))


def row_tiles(state, k, deep_s, deep_n, pair):
    rows = state.shape[2]
    level = k.astype(F32)
    tiles = []
    for f in (2 * pair, 2 * pair + 1):
        tiles.append(jnp.where(level < deep_s, state[f, k, 0:8, :], 0.0))
        tiles.append(jnp.where(level < deep_n, state[f, k, rows - 8:rows, :], 0.0))
    return join_rows(*tiles)


def join_rows(a_s, a_n, b_s, b_n):
    band_even = lax.axis_index("lat") % 2 == 0
    low = sublanes() < 4
    north = jnp.where(low, pltpu.roll(a_n, 4, 0), b_n)
    south = jnp.where(low, a_s, pltpu.roll(b_s, 4, 0))
    return jnp.where(band_even, north, south), jnp.where(band_even, south, north)


def far_kernel(state, depth, ra, p2):
    levels, rows = state.shape[1], state.shape[2]
    deep_s, deep_n = depth[4:12, :], depth[rows - 4:rows + 4, :]

    def body(k, unused):
        for pair in range(2):
            p2[2 * k + pair] = row_tiles(state, k, deep_s, deep_n, pair)[1]
        return unused

    lax.fori_loop(0, levels, body, 0, unroll=8)
    p2[2 * levels] = join_rows(deep_s, deep_n, deep_s, deep_n)[1]
    for f in range(4):
        for r in range(2):
            p2[2 * levels + 1, 2 * f + r:2 * f + r + 1, :] = edge_rows(ra, f, r)[1]
    for n in range(2 * levels + 2, p2.shape[0]):
        p2[n] = jnp.zeros((8, 128), F32)


def near_kernel(state, depth, ra, rb, p1):
    levels, rows = state.shape[1], state.shape[2]
    deep_s, deep_n = depth[4:12, :], depth[rows - 4:rows + 4, :]
    from_a = ((lanes()[0:1] & 3) < 2) == (lax.axis_index("lon") % 2 == 0)

    def body(k, unused):
        for pair in range(2):
            p1[2 * k + pair] = row_tiles(state, k, deep_s, deep_n, pair)[0]
        return unused

    lax.fori_loop(0, levels, body, 0, unroll=8)
    p1[2 * levels] = join_rows(deep_s, deep_n, deep_s, deep_n)[0]
    for f in range(4):
        for r in range(2):
            row = jnp.where(from_a, edge_rows(ra, f, r)[0], edge_rows(rb, f, r)[0])
            p1[2 * levels + 1, 2 * f + r:2 * f + r + 1, :] = row


def columns_kernel(state, depth, la, lb, cb):
    levels, rows = state.shape[1], state.shape[2]
    groups = rows // 8
    lon_even = lax.axis_index("lon") % 2 == 0
    zero = jnp.zeros((8, 128), F32)
    deeps = [depth[8 * g + 4:8 * g + 12, :] for g in range(groups)]
    group = lanes() >> 2
    for pair in range(2):
        def body(k, accs):
            level = k.astype(F32)
            spot_e = group == k
            spot_w = group == ((k + 1) & (levels - 1))
            new = []
            for j in range(2):
                for g in range(groups):
                    q = jnp.where(level < deeps[g], state[2 * pair + j, k, 8 * g:8 * g + 8, :], 0.0)
                    turned = pltpu.roll(q, (4 * k + 4) & 127, 1)
                    new.append(jnp.where(spot_e, turned, accs[len(new)]))
                    new.append(jnp.where(spot_w, turned, accs[len(new)]))
            return tuple(new)

        accs = lax.fori_loop(0, levels, body, (zero,) * (4 * groups), unroll=16)
        for j in range(2):
            for g in range(groups):
                at = slice(8 * g, 8 * g + 8)
                east, west = accs[2 * (j * groups + g)], accs[2 * (j * groups + g) + 1]
                la[2 * pair + j, at, :] = jnp.where(lon_even, east, west)
                lb[2 * pair + j, at, :] = jnp.where(lon_even, west, east)
    for g in range(groups):
        turned = pltpu.roll(deeps[g], 4, 1)
        la[4, 8 * g:8 * g + 8, :] = turned
        lb[4, 8 * g:8 * g + 8, :] = turned
    for f in range(4):
        for r in range(2):
            cb[2 * f + r:2 * f + r + 1, :] = edge_rows(lb, f, r)[1]


def coriolis_rows(first, total, order=None):
    row = first + (sublanes() if order is None else order)
    row = jnp.where(row >= total, 2 * total - 1 - row, row)
    return 0.2 + 0.8 * ((row.astype(F32) + 0.5) / total)


def sweep(table, levels, jobs, scale, leave=1.0, unroll=8, unroll_back=8):
    lane = lanes()
    zero = jnp.zeros((8, 128), F32)
    jobs = [job if len(job) == 9 else (*job, 1, job[2]) for job in jobs]
    turns = [cor * (UNIT * time_step * scale / DRIFT) for _, _, _, _, cor, *_ in jobs]
    uppers = [depth - 1.0 for _, _, _, depth, *_ in jobs]

    def forward(k, carry):
        inner, lowest = table[0, k], table[1, k]
        level = k.astype(F32)
        out = []
        for n, (own, other, o, depth, _, dst, d, apart, at) in enumerate(jobs):
            halves = carry[6 * n:6 * n + 4]
            sums = carry[6 * n + 4:6 * n + 6]
            weight = jnp.where(level < uppers[n], inner, jnp.where(level < depth, lowest, 0.0))
            q = [own[f, k, o:o + 8, :] for f in range(4)]
            cu = q[2] * (DRIFT / scale)
            cv = q[3] * (DRIFT / scale)
            prov = []
            near = []
            for f in range(4):
                x = other[f, k, at:at + 8, :]
                e1 = pltpu.roll(jnp.where(lane == 0, x, q[f]), 127, 1)
                e2 = pltpu.roll(jnp.where(lane < 2, x, q[f]), 126, 1)
                w1 = pltpu.roll(jnp.where(lane == 127, x, q[f]), 1, 1)
                w2 = pltpu.roll(jnp.where(lane >= 126, x, q[f]), 2, 1)
                n1 = own[f, k, o + apart:o + apart + 8, :]
                n2 = own[f, k, o + 2 * apart:o + 2 * apart + 8, :]
                s1 = own[f, k, o - apart:o - apart + 8, :]
                s2 = own[f, k, o - 2 * apart:o - 2 * apart + 8, :]
                dx, dy = e1 - w1, n1 - s1
                near.append((dx, dy))
                slope_x = 8.0 * dx - (e2 - w2)
                slope_y = 8.0 * dy - (n2 - s2)
                if f == 2:
                    slope_y = slope_y - turns[n]
                if f == 3:
                    slope_x = slope_x + turns[n]
                value = CENTRE * q[f] + ((e1 + w1) + (n1 + s1))
                prov.append(value - cu * slope_x - cv * slope_y)
            for axis in range(2):
                half = (PRESS * haline) * near[1][axis] - (PRESS * thermal) * near[0][axis]
                press = sums[axis] + half
                prov[2 + axis] = prov[2 + axis] - press
                near.append(press + half)
            for f in range(4):
                part = (prov[f] + halves[f]) * weight
                dst[f, k, d:d + 8, :] = part
                out.append(part)
            out += near[4:6]
        return tuple(out)

    lax.fori_loop(0, levels, forward, (zero,) * (6 * len(jobs)), unroll=unroll)

    def backward(step, carry):
        k = levels - 1 - step
        ratio = table[0, k]
        out = []
        for n, (_, _, _, _, _, dst, d, _, _) in enumerate(jobs):
            for f in range(4):
                value = dst[f, k, d:d + 8, :] + ratio * carry[4 * n + f]
                dst[f, k, d:d + 8, :] = value * leave if leave != 1.0 else value
                out.append(value)
        return tuple(out)

    lax.fori_loop(0, levels, backward, (zero,) * (4 * len(jobs)), unroll=unroll_back)


def side_tile(east, west, group, k):
    return pltpu.roll(jnp.where(group == k, west, east), (124 - 4 * k) & 127, 1)


def inner_kernel(state, depth, ra, rb, main0, side0, side1, main1, side_depth, last, easts, wests, table):
    levels, rows = state.shape[1], state.shape[2]
    groups = rows // 8
    lon_even = lax.axis_index("lon") % 2 == 0
    first_row = lax.axis_index("lat") * rows
    total = rows * lax.axis_size("lat")
    fill_table(table)
    group = lanes() >> 2
    zero = jnp.zeros((8, 128), F32)

    for f in range(5):
        for g in range(groups):
            at = slice(8 * g, 8 * g + 8)
            a, b = ra[f, at, :], rb[f, at, :]
            easts[f, at, :] = jnp.where(lon_even, a, b)
            wests[f, at, :] = jnp.where(lon_even, b, a)
    side_depth[0:8, :] = zero
    side_depth[rows:rows + 8, :] = zero
    for g in range(groups):
        at = slice(8 * g, 8 * g + 8)
        side_depth[8 * g + 4:8 * g + 12, :] = side_tile(easts[4, at, :], wests[4, at, :], group, 0)

    def fill(k, unused):
        level = k.astype(F32)
        for g in range(groups):
            at = slice(8 * g, 8 * g + 8)
            to = slice(8 * g + 4, 8 * g + 12)
            is_wet = level < depth[to, :]
            for f in range(4):
                main0[f, k, to, :] = jnp.where(is_wet, state[f, k, at, :], 0.0)
                side0[f, k, to, :] = side_tile(easts[f, at, :], wests[f, at, :], group, k)
        return unused

    lax.fori_loop(0, levels, fill, 0, unroll=16)

    jobs = []
    for w in range(1, groups):
        o = 8 * w + 2
        cor = coriolis_rows(first_row + (8 * w - 2), total)
        jobs.append((main0, side0, o, depth[o:o + 8, :], cor, main1, 8 * w))
        jobs.append((side0, main0, o, side_depth[o:o + 8, :], cor, side1, 8 * w))
    sweep(table, levels, jobs, 1.0, 1.0, 16, 8)
    jobs = []
    for w in range(1, groups - 1):
        cor = coriolis_rows(first_row + 8 * w, total)
        jobs.append((main1, side1, 8 * w + 2, depth[8 * w + 4:8 * w + 12, :], cor, last, 8 * w - 8))
    sweep(table, levels, jobs, GAIN, 1.0 / GAIN**2, 16, 8)


def south_kernel(p, depth, side_depth, main0, side0, main1, side1, last, rim0, edge0, rim1, edge1, table):
    levels = main0.shape[1]
    rows = depth.shape[0] - 8
    first_row = lax.axis_index("lat") * rows
    total = rows * lax.axis_size("lat")
    has_south = lax.axis_index("lat") > 0
    fill_table(table)
    corner = jnp.where(has_south, p[2 * levels + 1], 0.0)
    rim_depth = jnp.where(has_south, p[2 * levels], 0.0)
    depths = jnp.where(sublanes() < 2, pltpu.roll(rim_depth, 6, 0), depth[2:10, :])

    def fill(k, unused):
        corners = pltpu.roll(corner, (124 - 4 * k) & 127, 1)
        for pair in range(2):
            rim = jnp.where(has_south, p[2 * k + pair], 0.0)
            for j in range(2):
                f = 2 * pair + j
                rim0[f, k, 0:4, :] = rim[4 * j:4 * j + 4, :]
                rim0[f, k, 4:12, :] = main0[f, k, 4:12, :]
                edge0[f, k, 0:2, :] = jnp.zeros((2, 128), F32)
                edge0[f, k, 2:4, :] = corners[2 * f:2 * f + 2, :]
                edge0[f, k, 4:12, :] = side0[f, k, 4:12, :]
                rim1[f, k, 8:12, :] = main1[f, k, 8:12, :]
                edge1[f, k, 8:12, :] = side1[f, k, 8:12, :]
        return unused

    lax.fori_loop(0, levels, fill, 0, unroll=8)
    cor = coriolis_rows(first_row - 2, total)
    sweep(table, levels, [
        (rim0, edge0, 2, depths, cor, rim1, 0),
        (edge0, rim0, 2, side_depth[2:10, :], cor, edge1, 0),
    ], 1.0, 1.0, 16, 8)
    cor = coriolis_rows(first_row, total)
    sweep(table, levels, [(rim1, edge1, 2, depth[4:12, :], cor, last, 0)], GAIN, 1.0 / GAIN**2, 16, 8)


def north_kernel(p1, p2, cb, depth, side_depth, main0, side0, main1, side1, middle, south, out,
                 pair0, facing0, pair1, rim1, edge1, last, depths, table, sems):
    levels, rows = main0.shape[1], out.shape[2]
    done = [
        pltpu.make_async_copy(middle, out.at[:, :, 8:rows - 8, :], sems.at[0]),
        pltpu.make_async_copy(south, out.at[:, :, 0:8, :], sems.at[1]),
    ]
    for copy in done:
        copy.start()
    band = lax.axis_index("lat")
    band_even = band % 2 == 0
    first_row = band * rows
    total = rows * lax.axis_size("lat")
    is_top = band == lax.axis_size("lat") - 1
    fill_table(table)
    mirror = 127 - lanes()
    flip = sublanes() ^ 3

    def folded(tile):
        return jnp.take_along_axis(tile, mirror, axis=1, mode="promise_in_bounds")

    def ghost(index, sign):
        far = p2[index]
        turned = jnp.take_along_axis(folded(far), flip, axis=0, mode="promise_in_bounds") * sign
        return jnp.where(band_even, p1[index], jnp.where(is_top, turned, far))

    sender_even = (lax.axis_index("lon") % 2 == 0) != is_top
    far = jnp.where(((lanes() & 3) < 2) == sender_even, p2[2 * levels + 1], cb[...])
    turned = jnp.where(sublanes() < 4, folded(far), -folded(far))
    corner = jnp.where(band_even, p1[2 * levels + 1], jnp.where(is_top, turned, far))
    rim_depth = ghost(2 * levels, 1.0)

    def turns(start, count):
        return pl.ds(start, count, stride=2)

    depths[turns(0, 4), :] = side_depth[rows:rows + 4, :]
    depths[turns(1, 2), :] = depth[rows + 2:rows + 4, :]
    depths[turns(5, 2), :] = rim_depth[0:2, :]

    def fill(k, unused):
        corners = pltpu.roll(corner, jnp.where(is_top, 4 * k - 124, 124 - 4 * k) & 127, 1)
        for pair in range(2):
            rim = ghost(2 * k + pair, 1.0 if pair == 0 else -1.0)
            for j in range(2):
                f = 2 * pair + j
                pair0[f, k, turns(0, 6), :] = side0[f, k, rows - 2:rows + 4, :]
                pair0[f, k, turns(1, 4), :] = main0[f, k, rows:rows + 4, :]
                pair0[f, k, turns(9, 4), :] = rim[4 * j:4 * j + 4, :]
                pair0[f, k, turns(12, 2), :] = corners[2 * f:2 * f + 2, :]
                facing0[f, k, turns(0, 4), :] = main0[f, k, rows:rows + 4, :]
                facing0[f, k, turns(1, 2), :] = side0[f, k, rows + 2:rows + 4, :]
                facing0[f, k, turns(5, 2), :] = corners[2 * f:2 * f + 2, :]
        return unused

    lax.fori_loop(0, levels, fill, 0, unroll=8)
    cor = coriolis_rows(first_row + (rows - 4), total, (sublanes() >> 1) + 2 * (sublanes() & 1))
    sweep(table, levels, [(pair0, facing0, 4, depths[...], cor, pair1, 0, 2, 0)], 1.0, 1.0, 16, 8)

    def split(k, unused):
        for f in range(4):
            rim1[f, k, 0:8, :] = main1[f, k, rows - 8:rows, :]
            rim1[f, k, 8:12, :] = pair1[f, k, turns(1, 4), :]
            edge1[f, k, 0:4, :] = side1[f, k, rows - 6:rows - 2, :]
            edge1[f, k, 4:8, :] = pair1[f, k, turns(0, 4), :]
        return unused

    lax.fori_loop(0, levels, split, 0, unroll=8)
    cor = coriolis_rows(first_row + (rows - 8), total)
    sweep(table, levels, [(rim1, edge1, 2, depth[rows - 4:rows + 4, :], cor, last, 0, 1, 0)], GAIN, 1.0 / GAIN**2, 16, 8)
    copy = pltpu.make_async_copy(last, out.at[:, :, rows - 8:rows, :], sems.at[2])
    copy.start()
    for other in done:
        other.wait()
    copy.wait()


def per_device(state, land_mask, wet_levels):
    fields, levels, rows, cols = state.shape
    lon, lat = lax.axis_index("lon"), lax.axis_index("lat")
    count, bands = lax.axis_size("lon"), lax.axis_size("lat")

    def mate(i):
        return i ^ 1

    def beyond(i):
        return (i + 1) % count if i % 2 else (i - 1) % count

    def swap(x, to):
        pairs = []
        for i in range(count):
            for b in range(bands):
                ti, tb = to(i, b)
                pairs.append((i * bands + b, ti * bands + tb))
        return lax.ppermute(x, ("lon", "lat"), pairs)

    def near(i, b):
        return i, b ^ 1

    def far(i, b):
        if b == bands - 1:
            return count - 1 - i, b
        if b == 0:
            return i, b
        return i, (b + 1 if b % 2 else b - 1)

    def call(kernel, vmem, **given):
        return pl.pallas_call(kernel, compiler_params=pltpu.CompilerParams(vmem_limit_bytes=vmem * 2**20), **given)

    shape = lambda *dims: jax.ShapeDtypeStruct(dims, F32)
    block = lambda n: shape(fields, levels, n, 128)
    room = lambda n: pltpu.VMEM((fields, levels, n, 128), F32)
    strip = shape(5, rows, 128)
    top = call(
        functools.partial(limit_kernel, levels), 4, out_shape=shape(8, 128), out_specs=VM, name="limit",
        cost_estimate=pl.CostEstimate(flops=10**10, bytes_accessed=4096, transcendentals=0),
    )()
    depth = jnp.where(land_mask == 1, jnp.minimum(wet_levels.astype(F32), top[0]), 0.0)
    depth = jnp.pad(depth, ((4, 4), (0, 0)))
    la, lb, cb = call(
        columns_kernel, 4, out_shape=(strip, strip, shape(8, 128)), in_specs=[VM] * 2, out_specs=(VM,) * 3,
        name="columns",
    )(state, depth)
    ra = swap(la, lambda i, b: (mate(i), b))
    rb = swap(lb, lambda i, b: (beyond(i), b))
    rcb = swap(cb, lambda i, b: far(i if b == 0 else beyond(i), b))
    p2 = call(
        far_kernel, 4, out_shape=shape(2 * levels + 4, 8, 128), in_specs=[VM] * 3, out_specs=VM, name="far",
    )(state, depth, ra)
    rp2 = swap(p2, far)
    p1 = call(
        near_kernel, 4, out_shape=shape(2 * levels + 2, 8, 128), in_specs=[VM] * 4, out_specs=VM, name="near",
    )(state, depth, ra, rb)
    rp1 = swap(p1, near)
    south = rp1
    if bands > 2:
        same = jnp.where((jnp.arange(128) % 4 < 2) == (lon % 2 == 0), rp2[2 * levels + 1], rcb)
        south = jnp.where(lat % 2 == 0, rp2[:2 * levels + 2].at[2 * levels + 1].set(same), rp1)

    room_table = pltpu.SMEM((2, levels), F32)
    main0, side0, side1, main1, side_depth, last = call(
        inner_kernel,
        6,
        out_shape=(block(rows + 8), block(rows + 8), block(rows + 4), block(rows + 4), shape(rows + 8, 128),
                   block(rows - 16)),
        in_specs=[VM] * 4,
        out_specs=(VM,) * 6,
        scratch_shapes=[pltpu.VMEM((5, rows, 128), F32), pltpu.VMEM((5, rows, 128), F32), room_table],
        name="inner",
    )(state, depth, ra, rb)
    first = call(
        south_kernel,
        10,
        out_shape=block(8),
        in_specs=[VM] * 7,
        out_specs=VM,
        scratch_shapes=[room(16)] * 4 + [room_table],
        name="south",
    )(south, depth, side_depth, main0, side0, main1, side1)
    return call(
        north_kernel,
        12,
        out_shape=shape(*state.shape),
        in_specs=[VM] * 11,
        out_specs=HB,
        scratch_shapes=[room(16), room(8), room(8), room(16), room(8), room(8), pltpu.VMEM((8, 128), F32), room_table,
                        pltpu.SemaphoreType.DMA((3,))],
        name="north",
    )(rp1, rp2, rcb, depth, side_depth, main0, side0, main1, side1, last, first)


def solution(mesh):
    placed = (P(None, None, "lat", "lon"), P("lat", "lon"), P("lat", "lon"))
    return jax.shard_map(
        per_device,
        mesh=mesh,
        in_specs=placed,
        out_specs=P(None, None, "lat", "lon"),
        check_vma=False,
    )
```

```python
import functools

import jax
import jax.numpy as jnp
import numpy as np
from jax import lax
from jax.experimental import pallas as pl
from jax.experimental.pallas import tpu as pltpu
from jax.sharding import PartitionSpec as P

STEPS = 2
time_step = 0.1
lateral_mix = 0.5
column_mix = 0.5
gravity = 0.5
thermal = 0.2
haline = 0.8

F32 = jnp.float32
VM = pl.BlockSpec(memory_space=pltpu.VMEM)
HB = pl.BlockSpec(memory_space=pltpu.HBM)


UNIT = 1.0 / (time_step * lateral_mix)
GAIN = column_mix * UNIT
CENTRE = UNIT * (1.0 - 4.0 * time_step * lateral_mix)
DRIFT = UNIT * time_step / 12.0
PRESS = UNIT * time_step * 0.5 * gravity * 0.5


def factors(levels):
    inner = np.zeros(levels)
    lowest = np.zeros(levels)
    for k in range(levels):
        over = column_mix if k > 0 else 0.0
        less = column_mix * inner[k - 1] if k > 0 else 0.0
        inner[k] = column_mix / (1.0 + over + column_mix - less)
        lowest[k] = column_mix / (1.0 + over - less)
    return np.stack([inner, lowest]).astype(np.float32)


def fill_table(table):
    for n, row in enumerate(factors(table.shape[1])):
        for k, value in enumerate(row):
            table[n, k] = float(value)


def lanes():
    return lax.broadcasted_iota(jnp.int32, (8, 128), 1)


def sublanes():
    return lax.broadcasted_iota(jnp.int32, (8, 128), 0)


def limit_kernel(levels, top):
    top[...] = jnp.full(top.shape, float(levels), F32)


def edge_rows(strip, f, r):
    rows = strip.shape[1]
    band = lax.axis_index("lat")
    band_even = band % 2 == 0
    is_top = band == lax.axis_size("lat") - 1
    south, north = strip[f, r:r + 1, :], strip[f, rows - 2 + r:rows - 1 + r, :]
    folded = strip[f, rows - 1 - r:rows - r, :]
    return jnp.where(band_even, north, south), jnp.where(band_even, south, jnp.where(is_top, folded, north))


def row_tiles(state, k, deep_s, deep_n, pair):
    rows = state.shape[2]
    level = k.astype(F32)
    tiles = []
    for f in (2 * pair, 2 * pair + 1):
        tiles.append(jnp.where(level < deep_s, state[f, k, 0:8, :], 0.0))
        tiles.append(jnp.where(level < deep_n, state[f, k, rows - 8:rows, :], 0.0))
    return join_rows(*tiles)


def join_rows(a_s, a_n, b_s, b_n):
    band_even = lax.axis_index("lat") % 2 == 0
    low = sublanes() < 4
    north = jnp.where(low, pltpu.roll(a_n, 4, 0), b_n)
    south = jnp.where(low, a_s, pltpu.roll(b_s, 4, 0))
    return jnp.where(band_even, north, south), jnp.where(band_even, south, north)


def far_kernel(state, depth, ra, p2):
    levels, rows = state.shape[1], state.shape[2]
    deep_s, deep_n = depth[4:12, :], depth[rows - 4:rows + 4, :]

    def body(k, unused):
        for pair in range(2):
            p2[2 * k + pair] = row_tiles(state, k, deep_s, deep_n, pair)[1]
        return unused

    lax.fori_loop(0, levels, body, 0, unroll=8)
    p2[2 * levels] = join_rows(deep_s, deep_n, deep_s, deep_n)[1]
    for f in range(4):
        for r in range(2):
            p2[2 * levels + 1, 2 * f + r:2 * f + r + 1, :] = edge_rows(ra, f, r)[1]
    for n in range(2 * levels + 2, p2.shape[0]):
        p2[n] = jnp.zeros((8, 128), F32)


def near_kernel(state, depth, ra, rb, p1):
    levels, rows = state.shape[1], state.shape[2]
    deep_s, deep_n = depth[4:12, :], depth[rows - 4:rows + 4, :]
    from_a = ((lanes()[0:1] & 3) < 2) == (lax.axis_index("lon") % 2 == 0)

    def body(k, unused):
        for pair in range(2):
            p1[2 * k + pair] = row_tiles(state, k, deep_s, deep_n, pair)[0]
        return unused

    lax.fori_loop(0, levels, body, 0, unroll=8)
    p1[2 * levels] = join_rows(deep_s, deep_n, deep_s, deep_n)[0]
    for f in range(4):
        for r in range(2):
            row = jnp.where(from_a, edge_rows(ra, f, r)[0], edge_rows(rb, f, r)[0])
            p1[2 * levels + 1, 2 * f + r:2 * f + r + 1, :] = row


def columns_kernel(state, depth, la, lb, cb):
    levels, rows = state.shape[1], state.shape[2]
    groups = rows // 8
    lon_even = lax.axis_index("lon") % 2 == 0
    zero = jnp.zeros((8, 128), F32)
    deeps = [depth[8 * g + 4:8 * g + 12, :] for g in range(groups)]
    group = lanes() >> 2
    for pair in range(2):
        def body(k, accs):
            level = k.astype(F32)
            spot_e = group == k
            spot_w = group == ((k + 1) & (levels - 1))
            new = []
            for j in range(2):
                for g in range(groups):
                    q = jnp.where(level < deeps[g], state[2 * pair + j, k, 8 * g:8 * g + 8, :], 0.0)
                    turned = pltpu.roll(q, (4 * k + 4) & 127, 1)
                    new.append(jnp.where(spot_e, turned, accs[len(new)]))
                    new.append(jnp.where(spot_w, turned, accs[len(new)]))
            return tuple(new)

        accs = lax.fori_loop(0, levels, body, (zero,) * (4 * groups), unroll=32)
        for j in range(2):
            for g in range(groups):
                at = slice(8 * g, 8 * g + 8)
                east, west = accs[2 * (j * groups + g)], accs[2 * (j * groups + g) + 1]
                la[2 * pair + j, at, :] = jnp.where(lon_even, east, west)
                lb[2 * pair + j, at, :] = jnp.where(lon_even, west, east)
    for g in range(groups):
        turned = pltpu.roll(deeps[g], 4, 1)
        la[4, 8 * g:8 * g + 8, :] = turned
        lb[4, 8 * g:8 * g + 8, :] = turned
    for f in range(4):
        for r in range(2):
            cb[2 * f + r:2 * f + r + 1, :] = edge_rows(lb, f, r)[1]


def coriolis_rows(first, total, order=None):
    row = first + (sublanes() if order is None else order)
    row = jnp.where(row >= total, 2 * total - 1 - row, row)
    return 0.2 + 0.8 * ((row.astype(F32) + 0.5) / total)


def sweep(table, levels, jobs, scale, leave=1.0, unroll=8, unroll_back=8):
    lane = lanes()
    zero = jnp.zeros((8, 128), F32)
    jobs = [job if len(job) == 9 else (*job, 1, job[2]) for job in jobs]
    turns = [cor * (UNIT * time_step * scale / DRIFT) for _, _, _, _, cor, *_ in jobs]
    uppers = [depth - 1.0 for _, _, _, depth, *_ in jobs]

    def forward(k, carry):
        inner, lowest = table[0, k], table[1, k]
        level = k.astype(F32)
        out = []
        for n, (own, other, o, depth, _, dst, d, apart, at) in enumerate(jobs):
            halves = carry[6 * n:6 * n + 4]
            sums = carry[6 * n + 4:6 * n + 6]
            weight = jnp.where(level < uppers[n], inner, jnp.where(level < depth, lowest, 0.0))
            q = [own[f, k, o:o + 8, :] for f in range(4)]
            cu = q[2] * (DRIFT / scale)
            cv = q[3] * (DRIFT / scale)
            prov = []
            near = []
            for f in range(4):
                x = other[f, k, at:at + 8, :]
                e1 = pltpu.roll(jnp.where(lane == 0, x, q[f]), 127, 1)
                e2 = pltpu.roll(jnp.where(lane < 2, x, q[f]), 126, 1)
                w1 = pltpu.roll(jnp.where(lane == 127, x, q[f]), 1, 1)
                w2 = pltpu.roll(jnp.where(lane >= 126, x, q[f]), 2, 1)
                n1 = own[f, k, o + apart:o + apart + 8, :]
                n2 = own[f, k, o + 2 * apart:o + 2 * apart + 8, :]
                s1 = own[f, k, o - apart:o - apart + 8, :]
                s2 = own[f, k, o - 2 * apart:o - 2 * apart + 8, :]
                dx, dy = e1 - w1, n1 - s1
                near.append((dx, dy))
                slope_x = 8.0 * dx - (e2 - w2)
                slope_y = 8.0 * dy - (n2 - s2)
                if f == 2:
                    slope_y = slope_y - turns[n]
                if f == 3:
                    slope_x = slope_x + turns[n]
                value = CENTRE * q[f] + ((e1 + w1) + (n1 + s1))
                prov.append(value - cu * slope_x - cv * slope_y)
            for axis in range(2):
                half = (PRESS * haline) * near[1][axis] - (PRESS * thermal) * near[0][axis]
                press = sums[axis] + half
                prov[2 + axis] = prov[2 + axis] - press
                near.append(press + half)
            for f in range(4):
                part = (prov[f] + halves[f]) * weight
                dst[f, k, d:d + 8, :] = part
                out.append(part)
            out += near[4:6]
        return tuple(out)

    lax.fori_loop(0, levels, forward, (zero,) * (6 * len(jobs)), unroll=unroll)

    def backward(step, carry):
        k = levels - 1 - step
        ratio = table[0, k]
        out = []
        for n, (_, _, _, _, _, dst, d, _, _) in enumerate(jobs):
            for f in range(4):
                value = dst[f, k, d:d + 8, :] + ratio * carry[4 * n + f]
                dst[f, k, d:d + 8, :] = value * leave if leave != 1.0 else value
                out.append(value)
        return tuple(out)

    lax.fori_loop(0, levels, backward, (zero,) * (4 * len(jobs)), unroll=unroll_back)


def side_tile(east, west, group, k):
    return pltpu.roll(jnp.where(group == k, west, east), (124 - 4 * k) & 127, 1)


def inner_kernel(state, depth, ra, rb, main0, side0, side1, main1, side_depth, last, easts, wests, table):
    levels, rows = state.shape[1], state.shape[2]
    groups = rows // 8
    lon_even = lax.axis_index("lon") % 2 == 0
    first_row = lax.axis_index("lat") * rows
    total = rows * lax.axis_size("lat")
    fill_table(table)
    group = lanes() >> 2
    zero = jnp.zeros((8, 128), F32)

    for f in range(5):
        for g in range(groups):
            at = slice(8 * g, 8 * g + 8)
            a, b = ra[f, at, :], rb[f, at, :]
            easts[f, at, :] = jnp.where(lon_even, a, b)
            wests[f, at, :] = jnp.where(lon_even, b, a)
    side_depth[0:8, :] = zero
    side_depth[rows:rows + 8, :] = zero
    for g in range(groups):
        at = slice(8 * g, 8 * g + 8)
        side_depth[8 * g + 4:8 * g + 12, :] = side_tile(easts[4, at, :], wests[4, at, :], group, 0)

    def fill(k, unused):
        level = k.astype(F32)
        for g in range(groups):
            at = slice(8 * g, 8 * g + 8)
            to = slice(8 * g + 4, 8 * g + 12)
            is_wet = level < depth[to, :]
            for f in range(4):
                main0[f, k, to, :] = jnp.where(is_wet, state[f, k, at, :], 0.0)
                side0[f, k, to, :] = side_tile(easts[f, at, :], wests[f, at, :], group, k)
        return unused

    lax.fori_loop(0, levels, fill, 0, unroll=32)

    jobs = []
    for w in range(1, groups):
        o = 8 * w + 2
        cor = coriolis_rows(first_row + (8 * w - 2), total)
        jobs.append((main0, side0, o, depth[o:o + 8, :], cor, main1, 8 * w))
        jobs.append((side0, main0, o, side_depth[o:o + 8, :], cor, side1, 8 * w))
    sweep(table, levels, jobs, 1.0, 1.0, 16, 8)
    jobs = []
    for w in range(1, groups - 1):
        cor = coriolis_rows(first_row + 8 * w, total)
        jobs.append((main1, side1, 8 * w + 2, depth[8 * w + 4:8 * w + 12, :], cor, last, 8 * w - 8))
    sweep(table, levels, jobs, GAIN, 1.0 / GAIN**2, 32, 16)


def south_kernel(p, depth, side_depth, main0, side0, main1, side1, last, rim0, edge0, rim1, edge1, table):
    levels = main0.shape[1]
    rows = depth.shape[0] - 8
    first_row = lax.axis_index("lat") * rows
    total = rows * lax.axis_size("lat")
    has_south = lax.axis_index("lat") > 0
    fill_table(table)
    corner = jnp.where(has_south, p[2 * levels + 1], 0.0)
    rim_depth = jnp.where(has_south, p[2 * levels], 0.0)
    depths = jnp.where(sublanes() < 2, pltpu.roll(rim_depth, 6, 0), depth[2:10, :])

    def fill(k, unused):
        corners = pltpu.roll(corner, (124 - 4 * k) & 127, 1)
        for pair in range(2):
            rim = jnp.where(has_south, p[2 * k + pair], 0.0)
            for j in range(2):
                f = 2 * pair + j
                rim0[f, k, 0:4, :] = rim[4 * j:4 * j + 4, :]
                rim0[f, k, 4:12, :] = main0[f, k, 4:12, :]
                edge0[f, k, 0:2, :] = jnp.zeros((2, 128), F32)
                edge0[f, k, 2:4, :] = corners[2 * f:2 * f + 2, :]
                edge0[f, k, 4:12, :] = side0[f, k, 4:12, :]
                rim1[f, k, 8:12, :] = main1[f, k, 8:12, :]
                edge1[f, k, 8:12, :] = side1[f, k, 8:12, :]
        return unused

    lax.fori_loop(0, levels, fill, 0, unroll=32)
    cor = coriolis_rows(first_row - 2, total)
    sweep(table, levels, [
        (rim0, edge0, 2, depths, cor, rim1, 0),
        (edge0, rim0, 2, side_depth[2:10, :], cor, edge1, 0),
    ], 1.0, 1.0, 32, 16)
    cor = coriolis_rows(first_row, total)
    sweep(table, levels, [(rim1, edge1, 2, depth[4:12, :], cor, last, 0)], GAIN, 1.0 / GAIN**2, 32, 16)


def north_kernel(p1, p2, cb, own_cb, depth, side_depth, main0, side0, main1, side1, middle, south, out,
                 pair0, facing0, pair1, rim1, edge1, last, depths, table, sems):
    levels, rows = main0.shape[1], out.shape[2]
    done = [
        pltpu.make_async_copy(middle, out.at[:, :, 8:rows - 8, :], sems.at[0]),
        pltpu.make_async_copy(south, out.at[:, :, 0:8, :], sems.at[1]),
    ]
    for copy in done:
        copy.start()
    band = lax.axis_index("lat")
    band_even = band % 2 == 0
    first_row = band * rows
    total = rows * lax.axis_size("lat")
    is_top = band == lax.axis_size("lat") - 1
    fill_table(table)
    mirror = 127 - lanes()
    flip = sublanes() ^ 3

    def folded(tile):
        return jnp.take_along_axis(tile, mirror, axis=1, mode="promise_in_bounds")

    def ghost(index, sign):
        far = p2[index]
        turned = jnp.take_along_axis(folded(far), flip, axis=0, mode="promise_in_bounds") * sign
        return jnp.where(band_even, p1[index], jnp.where(is_top, turned, far))

    lon, count = lax.axis_index("lon"), lax.axis_size("lon")
    lon_even = lon % 2 == 0
    beyond = jnp.where(lon_even, lon + count - 1, lon + 1) % count
    beside = jnp.where(is_top & (lon + beyond == count - 1), own_cb[...], cb[...])
    far = jnp.where(((lanes() & 3) < 2) == (lon_even != is_top), p2[2 * levels + 1], beside)
    turned = jnp.where(sublanes() < 4, folded(far), -folded(far))
    corner = jnp.where(band_even, p1[2 * levels + 1], jnp.where(is_top, turned, far))
    rim_depth = ghost(2 * levels, 1.0)

    def turns(start, count):
        return pl.ds(start, count, stride=2)

    depths[turns(0, 4), :] = side_depth[rows:rows + 4, :]
    depths[turns(1, 2), :] = depth[rows + 2:rows + 4, :]
    depths[turns(5, 2), :] = rim_depth[0:2, :]

    def fill(k, unused):
        corners = pltpu.roll(corner, jnp.where(is_top, 4 * k - 124, 124 - 4 * k) & 127, 1)
        for pair in range(2):
            rim = ghost(2 * k + pair, 1.0 if pair == 0 else -1.0)
            for j in range(2):
                f = 2 * pair + j
                pair0[f, k, turns(0, 6), :] = side0[f, k, rows - 2:rows + 4, :]
                pair0[f, k, turns(1, 4), :] = main0[f, k, rows:rows + 4, :]
                pair0[f, k, turns(9, 4), :] = rim[4 * j:4 * j + 4, :]
                pair0[f, k, turns(12, 2), :] = corners[2 * f:2 * f + 2, :]
                facing0[f, k, turns(0, 4), :] = main0[f, k, rows:rows + 4, :]
                facing0[f, k, turns(1, 2), :] = side0[f, k, rows + 2:rows + 4, :]
                facing0[f, k, turns(5, 2), :] = corners[2 * f:2 * f + 2, :]
        return unused

    lax.fori_loop(0, levels, fill, 0, unroll=32)
    cor = coriolis_rows(first_row + (rows - 4), total, (sublanes() >> 1) + 2 * (sublanes() & 1))
    sweep(table, levels, [(pair0, facing0, 4, depths[...], cor, pair1, 0, 2, 0)], 1.0, 1.0, 32, 32)

    def split(k, unused):
        for f in range(4):
            rim1[f, k, 0:8, :] = main1[f, k, rows - 8:rows, :]
            rim1[f, k, 8:12, :] = pair1[f, k, turns(1, 4), :]
            edge1[f, k, 0:4, :] = side1[f, k, rows - 6:rows - 2, :]
            edge1[f, k, 4:8, :] = pair1[f, k, turns(0, 4), :]
        return unused

    lax.fori_loop(0, levels, split, 0, unroll=16)
    cor = coriolis_rows(first_row + (rows - 8), total)
    sweep(table, levels, [(rim1, edge1, 2, depth[rows - 4:rows + 4, :], cor, last, 0, 1, 0)], GAIN, 1.0 / GAIN**2, 32, 32)
    copy = pltpu.make_async_copy(last, out.at[:, :, rows - 8:rows, :], sems.at[2])
    copy.start()
    for other in done:
        other.wait()
    copy.wait()


def per_device(state, land_mask, wet_levels):
    fields, levels, rows, cols = state.shape
    lon, lat = lax.axis_index("lon"), lax.axis_index("lat")
    count, bands = lax.axis_size("lon"), lax.axis_size("lat")

    def mate(i):
        return i ^ 1

    def beyond(i):
        return (i + 1) % count if i % 2 else (i - 1) % count

    def swap(x, to):
        pairs = []
        for i in range(count):
            for b in range(bands):
                ti, tb = to(i, b)
                pairs.append((i * bands + b, ti * bands + tb))
        return lax.ppermute(x, ("lon", "lat"), pairs)

    def near(i, b):
        return i, b ^ 1

    def far(i, b):
        if b == bands - 1:
            return count - 1 - i, b
        if b == 0:
            return mate(i), b
        return i, (b + 1 if b % 2 else b - 1)

    def far_beyond(i, b):
        middle = count - 1 - beyond(i) == i
        if b in (0, bands - 1) and middle:
            return i, bands - 1 - b
        return far(beyond(i), b) if b else (beyond(i), b)

    def call(kernel, vmem, **given):
        return pl.pallas_call(kernel, compiler_params=pltpu.CompilerParams(vmem_limit_bytes=vmem * 2**20), **given)

    shape = lambda *dims: jax.ShapeDtypeStruct(dims, F32)
    block = lambda n: shape(fields, levels, n, 128)
    room = lambda n: pltpu.VMEM((fields, levels, n, 128), F32)
    strip = shape(5, rows, 128)
    top = call(
        functools.partial(limit_kernel, levels), 4, out_shape=shape(8, 128), out_specs=VM, name="limit",
        cost_estimate=pl.CostEstimate(flops=10**10, bytes_accessed=4096, transcendentals=0),
    )()
    depth = jnp.where(land_mask == 1, jnp.minimum(wet_levels.astype(F32), top[0]), 0.0)
    depth = jnp.pad(depth, ((4, 4), (0, 0)))
    la, lb, cb = call(
        columns_kernel, 4, out_shape=(strip, strip, shape(8, 128)), in_specs=[VM] * 2, out_specs=(VM,) * 3,
        name="columns",
    )(state, depth)
    ra = swap(la, lambda i, b: (mate(i), b))
    rb = swap(lb, lambda i, b: (beyond(i), b))
    rcb = swap(cb, far_beyond)
    p2 = call(
        far_kernel, 4, out_shape=shape(2 * levels + 4, 8, 128), in_specs=[VM] * 3, out_specs=VM, name="far",
    )(state, depth, ra)
    rp2 = swap(p2, far)
    p1 = call(
        near_kernel, 4, out_shape=shape(2 * levels + 2, 8, 128), in_specs=[VM] * 4, out_specs=VM, name="near",
    )(state, depth, ra, rb)
    rp1 = swap(p1, near)
    south = rp1
    if bands > 2:
        same = jnp.where((jnp.arange(128) % 4 < 2) == (lon % 2 == 0), rp2[2 * levels + 1], rcb)
        south = jnp.where(lat % 2 == 0, rp2[:2 * levels + 2].at[2 * levels + 1].set(same), rp1)

    room_table = pltpu.SMEM((2, levels), F32)
    main0, side0, side1, main1, side_depth, last = call(
        inner_kernel,
        6,
        out_shape=(block(rows + 8), block(rows + 8), block(rows + 4), block(rows + 4), shape(rows + 8, 128),
                   block(rows - 16)),
        in_specs=[VM] * 4,
        out_specs=(VM,) * 6,
        scratch_shapes=[pltpu.VMEM((5, rows, 128), F32), pltpu.VMEM((5, rows, 128), F32), room_table],
        name="inner",
    )(state, depth, ra, rb)
    first = call(
        south_kernel,
        10,
        out_shape=block(8),
        in_specs=[VM] * 7,
        out_specs=VM,
        scratch_shapes=[room(16)] * 4 + [room_table],
        name="south",
    )(south, depth, side_depth, main0, side0, main1, side1)
    return call(
        north_kernel,
        12,
        out_shape=shape(*state.shape),
        in_specs=[VM] * 12,
        out_specs=HB,
        scratch_shapes=[room(16), room(8), room(8), room(16), room(8), room(8), pltpu.VMEM((8, 128), F32), room_table,
                        pltpu.SemaphoreType.DMA((3,))],
        name="north",
    )(rp1, rp2, rcb, cb, depth, side_depth, main0, side0, main1, side1, last, first)


def solution(mesh):
    placed = (P(None, None, "lat", "lon"), P("lat", "lon"), P("lat", "lon"))
    return jax.shard_map(
        per_device,
        mesh=mesh,
        in_specs=placed,
        out_specs=P(None, None, "lat", "lon"),
        check_vma=False,
    )
```

```python
import functools

import jax
import jax.numpy as jnp
import numpy as np
from jax import lax
from jax.experimental import pallas as pl
from jax.experimental.pallas import tpu as pltpu
from jax.sharding import PartitionSpec as P

STEPS = 2
time_step = 0.1
lateral_mix = 0.5
column_mix = 0.5
gravity = 0.5
thermal = 0.2
haline = 0.8

F32 = jnp.float32
PARTS = 4
VM = pl.BlockSpec(memory_space=pltpu.VMEM)
HB = pl.BlockSpec(memory_space=pltpu.HBM)


UNIT = 1.0 / (time_step * lateral_mix)
GAIN = column_mix * UNIT
CENTRE = UNIT * (1.0 - 4.0 * time_step * lateral_mix)
DRIFT = UNIT * time_step / 12.0
PRESS = UNIT * time_step * 0.5 * gravity * 0.5


def factors(levels):
    inner = np.zeros(levels)
    lowest = np.zeros(levels)
    for k in range(levels):
        over = column_mix if k > 0 else 0.0
        less = column_mix * inner[k - 1] if k > 0 else 0.0
        inner[k] = column_mix / (1.0 + over + column_mix - less)
        lowest[k] = column_mix / (1.0 + over - less)
    return np.stack([inner, lowest]).astype(np.float32)


def fill_table(table):
    for n, row in enumerate(factors(table.shape[1])):
        for k, value in enumerate(row):
            table[n, k] = float(value)


def lanes():
    return lax.broadcasted_iota(jnp.int32, (8, 128), 1)


def sublanes():
    return lax.broadcasted_iota(jnp.int32, (8, 128), 0)


def limit_kernel(levels, top):
    top[...] = jnp.full(top.shape, float(levels), F32)


def edge_rows(strip, f, r):
    rows = (strip.shape[0] - 8) // 4
    base = f * rows
    band = lax.axis_index("lat")
    band_even = band % 2 == 0
    is_top = band == lax.axis_size("lat") - 1
    south, north = strip[base + r:base + r + 1, :], strip[base + rows - 2 + r:base + rows - 1 + r, :]
    folded = strip[base + rows - 1 - r:base + rows - r, :]
    return jnp.where(band_even, north, south), jnp.where(band_even, south, jnp.where(is_top, folded, north))


def row_tiles(state, k, deep_s, deep_n, pair):
    rows = state.shape[2]
    level = k.astype(F32)
    tiles = []
    for f in (2 * pair, 2 * pair + 1):
        tiles.append(jnp.where(level < deep_s, state[f, k, 0:8, :], 0.0))
        tiles.append(jnp.where(level < deep_n, state[f, k, rows - 8:rows, :], 0.0))
    return join_rows(*tiles)


def join_rows(a_s, a_n, b_s, b_n):
    band_even = lax.axis_index("lat") % 2 == 0
    low = sublanes() < 4
    north = jnp.where(low, pltpu.roll(a_n, 4, 0), b_n)
    south = jnp.where(low, a_s, pltpu.roll(b_s, 4, 0))
    return jnp.where(band_even, north, south), jnp.where(band_even, south, north)


def far_kernel(state, depth, ra, p2):
    levels, rows = state.shape[1], state.shape[2]
    deep_s, deep_n = depth[4:12, :], depth[rows - 4:rows + 4, :]

    def body(k, unused):
        for pair in range(2):
            p2[2 * k + pair] = row_tiles(state, k, deep_s, deep_n, pair)[1]
        return unused

    lax.fori_loop(0, levels, body, 0, unroll=8)
    p2[2 * levels] = join_rows(deep_s, deep_n, deep_s, deep_n)[1]
    for f in range(4):
        for r in range(2):
            p2[2 * levels + 1, 2 * f + r:2 * f + r + 1, :] = edge_rows(ra, f, r)[1]
    for n in range(2 * levels + 2, p2.shape[0]):
        p2[n] = jnp.zeros((8, 128), F32)


def near_kernel(state, depth, ra, rb, p1):
    levels, rows = state.shape[1], state.shape[2]
    deep_s, deep_n = depth[4:12, :], depth[rows - 4:rows + 4, :]
    from_a = ((lanes()[0:1] & 3) < 2) == (lax.axis_index("lon") % 2 == 0)

    def body(k, unused):
        for pair in range(2):
            p1[2 * k + pair] = row_tiles(state, k, deep_s, deep_n, pair)[0]
        return unused

    lax.fori_loop(0, levels, body, 0, unroll=8)
    p1[2 * levels] = join_rows(deep_s, deep_n, deep_s, deep_n)[0]
    for f in range(4):
        for r in range(2):
            row = jnp.where(from_a, edge_rows(ra, f, r)[0], edge_rows(rb, f, r)[0])
            p1[2 * levels + 1, 2 * f + r:2 * f + r + 1, :] = row


def columns_kernel(state, depth, la, lb, cb):
    levels, rows = state.shape[1], state.shape[2]
    groups = rows // 8
    lon_even = lax.axis_index("lon") % 2 == 0
    zero = jnp.zeros((8, 128), F32)
    deeps = [depth[8 * g + 4:8 * g + 12, :] for g in range(groups)]
    group = lanes() >> 2
    for pair in range(2):
        def body(k, accs):
            level = k.astype(F32)
            spot_e = group == k
            spot_w = group == ((k + 1) & (levels - 1))
            new = []
            for j in range(2):
                for g in range(groups):
                    q = jnp.where(level < deeps[g], state[2 * pair + j, k, 8 * g:8 * g + 8, :], 0.0)
                    turned = pltpu.roll(q, (4 * k + 4) & 127, 1)
                    new.append(jnp.where(spot_e, turned, accs[len(new)]))
                    new.append(jnp.where(spot_w, turned, accs[len(new)]))
            return tuple(new)

        accs = lax.fori_loop(0, levels, body, (zero,) * (4 * groups), unroll=32)
        for j in range(2):
            for g in range(groups):
                at = slice((2 * pair + j) * rows + 8 * g, (2 * pair + j) * rows + 8 * g + 8)
                east, west = accs[2 * (j * groups + g)], accs[2 * (j * groups + g) + 1]
                la[at, :] = jnp.where(lon_even, east, west)
                lb[at, :] = jnp.where(lon_even, west, east)
    east = west = zero
    for g in range(groups):
        turned = pltpu.roll(deeps[g], 4 * g + 4, 1)
        east = jnp.where(group == g, turned, east)
        west = jnp.where(group == g + 1, turned, west)
    la[4 * rows:4 * rows + 8, :] = jnp.where(lon_even, east, west)
    lb[4 * rows:4 * rows + 8, :] = jnp.where(lon_even, west, east)
    for f in range(4):
        for r in range(2):
            cb[2 * f + r:2 * f + r + 1, :] = edge_rows(lb, f, r)[1]


def coriolis_rows(first, total, order=None):
    row = first + (sublanes() if order is None else order)
    row = jnp.where(row >= total, 2 * total - 1 - row, row)
    return 0.2 + 0.8 * ((row.astype(F32) + 0.5) / total)


def sweep(table, levels, jobs, scale, leave=1.0, unroll=8, unroll_back=8, parts=1, ready=None):
    lane = lanes()
    zero = jnp.zeros((8, 128), F32)
    jobs = [job if len(job) == 9 else (*job, 1, job[2]) for job in jobs]
    turns = [cor * (UNIT * time_step * scale / DRIFT) for _, _, _, _, cor, *_ in jobs]
    uppers = [depth - 1.0 for _, _, _, depth, *_ in jobs]

    def forward(k, carry):
        inner, lowest = table[0, k], table[1, k]
        level = k.astype(F32)
        out = []
        for n, (own, other, o, depth, _, dst, d, apart, at) in enumerate(jobs):
            halves = carry[6 * n:6 * n + 4]
            sums = carry[6 * n + 4:6 * n + 6]
            weight = jnp.where(level < uppers[n], inner, jnp.where(level < depth, lowest, 0.0))
            q = [own[f, k, o:o + 8, :] for f in range(4)]
            cu = q[2] * (DRIFT / scale)
            cv = q[3] * (DRIFT / scale)
            prov = []
            near = []
            for f in range(4):
                x = other(f, k) if callable(other) else other[f, k, at:at + 8, :]
                e1 = pltpu.roll(jnp.where(lane == 0, x, q[f]), 127, 1)
                e2 = pltpu.roll(jnp.where(lane < 2, x, q[f]), 126, 1)
                w1 = pltpu.roll(jnp.where(lane == 127, x, q[f]), 1, 1)
                w2 = pltpu.roll(jnp.where(lane >= 126, x, q[f]), 2, 1)
                n1 = own[f, k, o + apart:o + apart + 8, :]
                n2 = own[f, k, o + 2 * apart:o + 2 * apart + 8, :]
                s1 = own[f, k, o - apart:o - apart + 8, :]
                s2 = own[f, k, o - 2 * apart:o - 2 * apart + 8, :]
                dx, dy = e1 - w1, n1 - s1
                near.append((dx, dy))
                slope_x = 8.0 * dx - (e2 - w2)
                slope_y = 8.0 * dy - (n2 - s2)
                if f == 2:
                    slope_y = slope_y - turns[n]
                if f == 3:
                    slope_x = slope_x + turns[n]
                value = CENTRE * q[f] + ((e1 + w1) + (n1 + s1))
                prov.append(value - cu * slope_x - cv * slope_y)
            for axis in range(2):
                half = (PRESS * haline) * near[1][axis] - (PRESS * thermal) * near[0][axis]
                press = sums[axis] + half
                prov[2 + axis] = prov[2 + axis] - press
                near.append(press + half)
            for f in range(4):
                part = (prov[f] + halves[f]) * weight
                dst[f, k, d:d + 8, :] = part
                out.append(part)
            out += near[4:6]
        return tuple(out)

    lax.fori_loop(0, levels, forward, (zero,) * (6 * len(jobs)), unroll=unroll)

    def backward(step, carry):
        k = levels - 1 - step
        ratio = table[0, k]
        out = []
        for n, (_, _, _, _, _, dst, d, _, _) in enumerate(jobs):
            for f in range(4):
                value = dst[f, k, d:d + 8, :] + ratio * carry[4 * n + f]
                dst[f, k, d:d + 8, :] = value * leave if leave != 1.0 else value
                out.append(value)
        return tuple(out)

    carry = (zero,) * (4 * len(jobs))
    size = levels // parts
    for n in range(parts):
        carry = lax.fori_loop(n * size, (n + 1) * size, backward, carry, unroll=min(unroll_back, size))
        if ready is not None:
            ready(n, levels - (n + 1) * size, size)


def side_tile(east, west, group, k):
    return pltpu.roll(jnp.where(group == k, west, east), (124 - 4 * k) & 127, 1)


def inner_kernel(state, depth, ra, rb, main0, side0, side1, main1, side_depth, last, easts, wests, table):
    levels, rows = state.shape[1], state.shape[2]
    groups = rows // 8
    lon_even = lax.axis_index("lon") % 2 == 0
    first_row = lax.axis_index("lat") * rows
    total = rows * lax.axis_size("lat")
    fill_table(table)
    group = lanes() >> 2
    zero = jnp.zeros((8, 128), F32)

    for n in range(ra.shape[0] // 8):
        at = slice(8 * n, 8 * n + 8)
        a, b = ra[at, :], rb[at, :]
        easts[at, :] = jnp.where(lon_even, a, b)
        wests[at, :] = jnp.where(lon_even, b, a)
    side_depth[0:8, :] = zero
    side_depth[rows:rows + 8, :] = zero
    for g in range(groups):
        at = slice(4 * rows, 4 * rows + 8)
        side_depth[8 * g + 4:8 * g + 12, :] = side_tile(easts[at, :], wests[at, :], group, g)

    def fill(k, unused):
        level = k.astype(F32)
        for g in range(groups):
            at = slice(8 * g, 8 * g + 8)
            to = slice(8 * g + 4, 8 * g + 12)
            is_wet = level < depth[to, :]
            for f in range(4):
                main0[f, k, to, :] = jnp.where(is_wet, state[f, k, at, :], 0.0)
                of = slice(f * rows + 8 * g, f * rows + 8 * g + 8)
                side0[f, k, to, :] = side_tile(easts[of, :], wests[of, :], group, k)
        return unused

    lax.fori_loop(0, levels, fill, 0, unroll=32)

    jobs = []
    for w in range(1, groups):
        o = 8 * w + 2
        cor = coriolis_rows(first_row + (8 * w - 2), total)
        jobs.append((main0, side0, o, depth[o:o + 8, :], cor, main1, 8 * w))
        jobs.append((side0, main0, o, side_depth[o:o + 8, :], cor, side1, 8 * w))
    sweep(table, levels, jobs, 1.0, 1.0, 16, 8)
    jobs = []
    for w in range(1, groups - 1):
        cor = coriolis_rows(first_row + 8 * w, total)
        jobs.append((main1, side1, 8 * w + 2, depth[8 * w + 4:8 * w + 12, :], cor, last, 8 * w - 8))
    sweep(table, levels, jobs, GAIN, 1.0 / GAIN**2, 32, 16)


def south_kernel(p, depth, side_depth, main0, side0, main1, side1, last, rim0, edge0, rim1, edge1, table):
    levels = main0.shape[1]
    rows = depth.shape[0] - 8
    first_row = lax.axis_index("lat") * rows
    total = rows * lax.axis_size("lat")
    has_south = lax.axis_index("lat") > 0
    fill_table(table)
    corner = jnp.where(has_south, p[2 * levels + 1], 0.0)
    rim_depth = jnp.where(has_south, p[2 * levels], 0.0)
    depths = jnp.where(sublanes() < 2, pltpu.roll(rim_depth, 6, 0), depth[2:10, :])

    def fill(k, unused):
        corners = pltpu.roll(corner, (124 - 4 * k) & 127, 1)
        for pair in range(2):
            rim = jnp.where(has_south, p[2 * k + pair], 0.0)
            for j in range(2):
                f = 2 * pair + j
                rim0[f, k, 0:4, :] = rim[4 * j:4 * j + 4, :]
                rim0[f, k, 4:12, :] = main0[f, k, 4:12, :]
                edge0[f, k, 0:2, :] = jnp.zeros((2, 128), F32)
                edge0[f, k, 2:4, :] = corners[2 * f:2 * f + 2, :]
                edge0[f, k, 4:12, :] = side0[f, k, 4:12, :]
                rim1[f, k, 8:12, :] = main1[f, k, 8:12, :]
                edge1[f, k, 8:12, :] = side1[f, k, 8:12, :]
        return unused

    lax.fori_loop(0, levels, fill, 0, unroll=32)
    cor = coriolis_rows(first_row - 2, total)
    sweep(table, levels, [
        (rim0, edge0, 2, depths, cor, rim1, 0),
        (edge0, rim0, 2, side_depth[2:10, :], cor, edge1, 0),
    ], 1.0, 1.0, 32, 16)
    cor = coriolis_rows(first_row, total)
    sweep(table, levels, [(rim1, edge1, 2, depth[4:12, :], cor, last, 0)], GAIN, 1.0 / GAIN**2, 32, 16)


def north_kernel(p1, p2, cb, own_cb, depth, side_depth, main0, side0, main1, side1, middle, south, out,
                 pair0, pair1, rim1, edge1, last, depths, table, sems):
    levels, rows = main0.shape[1], out.shape[2]
    done = [
        pltpu.make_async_copy(middle, out.at[:, :, 8:rows - 8, :], sems.at[0]),
        pltpu.make_async_copy(south, out.at[:, :, 0:8, :], sems.at[1]),
    ]
    for copy in done:
        copy.start()
    band = lax.axis_index("lat")
    band_even = band % 2 == 0
    first_row = band * rows
    total = rows * lax.axis_size("lat")
    is_top = band == lax.axis_size("lat") - 1
    fill_table(table)
    mirror = 127 - lanes()
    flip = sublanes() ^ 3

    def folded(tile):
        return jnp.take_along_axis(tile, mirror, axis=1, mode="promise_in_bounds")

    def ghost(index, sign):
        far = p2[index]
        turned = jnp.take_along_axis(folded(far), flip, axis=0, mode="promise_in_bounds") * sign
        return jnp.where(band_even, p1[index], jnp.where(is_top, turned, far))

    lon, count = lax.axis_index("lon"), lax.axis_size("lon")
    lon_even = lon % 2 == 0
    beyond = jnp.where(lon_even, lon + count - 1, lon + 1) % count
    beside = jnp.where(is_top & (lon + beyond == count - 1), own_cb[...], cb[...])
    far = jnp.where(((lanes() & 3) < 2) == (lon_even != is_top), p2[2 * levels + 1], beside)
    turned = jnp.where(sublanes() < 4, folded(far), -folded(far))
    corner = jnp.where(band_even, p1[2 * levels + 1], jnp.where(is_top, turned, far))
    rim_depth = ghost(2 * levels, 1.0)

    def turns(start, count):
        return pl.ds(start, count, stride=2)

    depths[turns(0, 4), :] = side_depth[rows:rows + 4, :]
    depths[turns(1, 2), :] = depth[rows + 2:rows + 4, :]
    depths[turns(5, 2), :] = rim_depth[0:2, :]

    def fill(k, unused):
        corners = pltpu.roll(corner, jnp.where(is_top, 4 * k - 124, 124 - 4 * k) & 127, 1)
        for pair in range(2):
            rim = ghost(2 * k + pair, 1.0 if pair == 0 else -1.0)
            for j in range(2):
                f = 2 * pair + j
                pair0[f, k, turns(0, 6), :] = side0[f, k, rows - 2:rows + 4, :]
                pair0[f, k, turns(1, 4), :] = main0[f, k, rows:rows + 4, :]
                pair0[f, k, turns(9, 4), :] = rim[4 * j:4 * j + 4, :]
                pair0[f, k, turns(12, 2), :] = corners[2 * f:2 * f + 2, :]
        return unused

    lax.fori_loop(0, levels, fill, 0, unroll=32)
    cor = coriolis_rows(first_row + (rows - 4), total, (sublanes() >> 1) + 2 * (sublanes() & 1))
    first_turn = sublanes() & 1 == 0

    def facing(f, k):
        return jnp.where(first_turn, pair0[f, k, 1:9, :], pair0[f, k, 7:15, :])

    sweep(table, levels, [(pair0, facing, 4, depths[...], cor, pair1, 0, 2, 0)], 1.0, 1.0, 32, 32)

    def split(k, unused):
        for f in range(4):
            rim1[f, k, 0:8, :] = main1[f, k, rows - 8:rows, :]
            rim1[f, k, 8:12, :] = pair1[f, k, turns(1, 4), :]
            edge1[f, k, 0:4, :] = side1[f, k, rows - 6:rows - 2, :]
            edge1[f, k, 4:8, :] = pair1[f, k, turns(0, 4), :]
        return unused

    lax.fori_loop(0, levels, split, 0, unroll=16)
    cor = coriolis_rows(first_row + (rows - 8), total)

    def send(n, k, size):
        done.append(pltpu.make_async_copy(
            last.at[:, k:k + size], out.at[:, k:k + size, rows - 8:rows, :], sems.at[2 + n]))
        done[-1].start()

    sweep(table, levels, [(rim1, edge1, 2, depth[rows - 4:rows + 4, :], cor, last, 0, 1, 0)],
          GAIN, 1.0 / GAIN**2, 32, 32, PARTS, send)
    for copy in done:
        copy.wait()


def per_device(state, land_mask, wet_levels):
    fields, levels, rows, cols = state.shape
    lon, lat = lax.axis_index("lon"), lax.axis_index("lat")
    count, bands = lax.axis_size("lon"), lax.axis_size("lat")

    def mate(i):
        return i ^ 1

    def beyond(i):
        return (i + 1) % count if i % 2 else (i - 1) % count

    def swap(x, to):
        pairs = []
        for i in range(count):
            for b in range(bands):
                ti, tb = to(i, b)
                pairs.append((i * bands + b, ti * bands + tb))
        return lax.ppermute(x, ("lon", "lat"), pairs)

    def near(i, b):
        return i, b ^ 1

    def far(i, b):
        if b == bands - 1:
            return count - 1 - i, b
        if b == 0:
            return mate(i), b
        return i, (b + 1 if b % 2 else b - 1)

    def far_beyond(i, b):
        middle = count - 1 - beyond(i) == i
        if b in (0, bands - 1) and middle:
            return i, bands - 1 - b
        return far(beyond(i), b) if b else (beyond(i), b)

    def call(kernel, vmem, **given):
        return pl.pallas_call(kernel, compiler_params=pltpu.CompilerParams(vmem_limit_bytes=vmem * 2**20), **given)

    shape = lambda *dims: jax.ShapeDtypeStruct(dims, F32)
    block = lambda n: shape(fields, levels, n, 128)
    room = lambda n: pltpu.VMEM((fields, levels, n, 128), F32)
    strip = shape(4 * rows + 8, 128)
    top = call(
        functools.partial(limit_kernel, levels), 4, out_shape=shape(8, 128), out_specs=VM, name="limit",
        cost_estimate=pl.CostEstimate(flops=10**10, bytes_accessed=4096, transcendentals=0),
    )()
    depth = jnp.where(land_mask == 1, jnp.minimum(wet_levels.astype(F32), top[0]), 0.0)
    depth = jnp.pad(depth, ((4, 4), (0, 0)))
    la, lb, cb = call(
        columns_kernel, 4, out_shape=(strip, strip, shape(8, 128)), in_specs=[VM] * 2, out_specs=(VM,) * 3,
        name="columns",
    )(state, depth)
    ra = swap(la, lambda i, b: (mate(i), b))
    rb = swap(lb, lambda i, b: (beyond(i), b))
    rcb = swap(cb, far_beyond)
    p2 = call(
        far_kernel, 4, out_shape=shape(2 * levels + 3, 8, 128), in_specs=[VM] * 3, out_specs=VM, name="far",
    )(state, depth, ra)
    rp2 = swap(p2, far)
    p1 = call(
        near_kernel, 4, out_shape=shape(2 * levels + 2, 8, 128), in_specs=[VM] * 4, out_specs=VM, name="near",
    )(state, depth, ra, rb)
    rp1 = swap(p1, near)
    south = rp1
    if bands > 2:
        same = jnp.where((jnp.arange(128) % 4 < 2) == (lon % 2 == 0), rp2[2 * levels + 1], rcb)
        south = jnp.where(lat % 2 == 0, rp2[:2 * levels + 2].at[2 * levels + 1].set(same), rp1)

    room_table = pltpu.SMEM((2, levels), F32)
    main0, side0, side1, main1, side_depth, last = call(
        inner_kernel,
        6,
        out_shape=(block(rows + 8), block(rows + 8), block(rows + 4), block(rows + 4), shape(rows + 8, 128),
                   block(rows - 16)),
        in_specs=[VM] * 4,
        out_specs=(VM,) * 6,
        scratch_shapes=[pltpu.VMEM((4 * rows + 8, 128), F32), pltpu.VMEM((4 * rows + 8, 128), F32), room_table],
        name="inner",
    )(state, depth, ra, rb)
    first = call(
        south_kernel,
        10,
        out_shape=block(8),
        in_specs=[VM] * 7,
        out_specs=VM,
        scratch_shapes=[room(16)] * 4 + [room_table],
        name="south",
    )(south, depth, side_depth, main0, side0, main1, side1)
    return call(
        north_kernel,
        12,
        out_shape=shape(*state.shape),
        in_specs=[VM] * 12,
        out_specs=HB,
        scratch_shapes=[room(16), room(8), room(16), room(8), room(8), pltpu.VMEM((8, 128), F32), room_table,
                        pltpu.SemaphoreType.DMA((2 + PARTS,))],
        name="north",
    )(rp1, rp2, rcb, cb, depth, side_depth, main0, side0, main1, side1, last, first)


def solution(mesh):
    placed = (P(None, None, "lat", "lon"), P("lat", "lon"), P("lat", "lon"))
    return jax.shard_map(
        per_device,
        mesh=mesh,
        in_specs=placed,
        out_specs=P(None, None, "lat", "lon"),
        check_vma=False,
    )
```

```python
import functools

import jax
import jax.numpy as jnp
import numpy as np
from jax import lax
from jax.experimental import pallas as pl
from jax.experimental.pallas import tpu as pltpu
from jax.sharding import PartitionSpec as P

STEPS = 2
time_step = 0.1
lateral_mix = 0.5
column_mix = 0.5
gravity = 0.5
thermal = 0.2
haline = 0.8

F32 = jnp.float32
PARTS = 4
VM = pl.BlockSpec(memory_space=pltpu.VMEM)
HB = pl.BlockSpec(memory_space=pltpu.HBM)


UNIT = 1.0 / (time_step * lateral_mix)
GAIN = column_mix * UNIT
CENTRE = UNIT * (1.0 - 4.0 * time_step * lateral_mix)
DRIFT = UNIT * time_step / 12.0
PRESS = UNIT * time_step * 0.5 * gravity * 0.5


def factors(levels):
    inner = np.zeros(levels)
    lowest = np.zeros(levels)
    for k in range(levels):
        over = column_mix if k > 0 else 0.0
        less = column_mix * inner[k - 1] if k > 0 else 0.0
        inner[k] = column_mix / (1.0 + over + column_mix - less)
        lowest[k] = column_mix / (1.0 + over - less)
    return np.stack([inner, lowest]).astype(np.float32)


def fill_table(table):
    for n, row in enumerate(factors(table.shape[1])):
        for k, value in enumerate(row):
            table[n, k] = float(value)


def lanes():
    return lax.broadcasted_iota(jnp.int32, (8, 128), 1)


def sublanes():
    return lax.broadcasted_iota(jnp.int32, (8, 128), 0)


def limit_kernel(levels, top):
    top[...] = jnp.full(top.shape, float(levels), F32)


def edge_rows(strip, f, r):
    rows = (strip.shape[0] - 8) // 4
    base = f * rows
    band = lax.axis_index("lat")
    band_even = band % 2 == 0
    is_top = band == lax.axis_size("lat") - 1
    south, north = strip[base + r:base + r + 1, :], strip[base + rows - 2 + r:base + rows - 1 + r, :]
    folded = strip[base + rows - 1 - r:base + rows - r, :]
    return jnp.where(band_even, north, south), jnp.where(band_even, south, jnp.where(is_top, folded, north))


def row_tiles(state, k, deep_s, deep_n, pair):
    rows = state.shape[2]
    level = k.astype(F32)
    tiles = []
    for f in (2 * pair, 2 * pair + 1):
        tiles.append(jnp.where(level < deep_s, state[f, k, 0:8, :], 0.0))
        tiles.append(jnp.where(level < deep_n, state[f, k, rows - 8:rows, :], 0.0))
    return join_rows(*tiles)


def join_rows(a_s, a_n, b_s, b_n):
    band_even = lax.axis_index("lat") % 2 == 0
    low = sublanes() < 4
    north = jnp.where(low, pltpu.roll(a_n, 4, 0), b_n)
    south = jnp.where(low, a_s, pltpu.roll(b_s, 4, 0))
    return jnp.where(band_even, north, south), jnp.where(band_even, south, north)


def far_kernel(state, depth, ra, p2):
    levels, rows = state.shape[1], state.shape[2]
    deep_s, deep_n = depth[4:12, :], depth[rows - 4:rows + 4, :]

    def body(k, unused):
        for pair in range(2):
            p2[2 * k + pair] = row_tiles(state, k, deep_s, deep_n, pair)[1]
        return unused

    lax.fori_loop(0, levels, body, 0, unroll=8)
    p2[2 * levels] = join_rows(deep_s, deep_n, deep_s, deep_n)[1]
    for f in range(4):
        for r in range(2):
            p2[2 * levels + 1, 2 * f + r:2 * f + r + 1, :] = edge_rows(ra, f, r)[1]
    for n in range(2 * levels + 2, p2.shape[0]):
        p2[n] = jnp.zeros((8, 128), F32)


def near_kernel(state, depth, ra, rb, p1):
    levels, rows = state.shape[1], state.shape[2]
    deep_s, deep_n = depth[4:12, :], depth[rows - 4:rows + 4, :]
    from_a = ((lanes()[0:1] & 3) < 2) == (lax.axis_index("lon") % 2 == 0)

    def body(k, unused):
        for pair in range(2):
            p1[2 * k + pair] = row_tiles(state, k, deep_s, deep_n, pair)[0]
        return unused

    lax.fori_loop(0, levels, body, 0, unroll=8)
    p1[2 * levels] = join_rows(deep_s, deep_n, deep_s, deep_n)[0]
    for f in range(4):
        for r in range(2):
            row = jnp.where(from_a, edge_rows(ra, f, r)[0], edge_rows(rb, f, r)[0])
            p1[2 * levels + 1, 2 * f + r:2 * f + r + 1, :] = row


def columns_kernel(state, depth, la, lb, cb):
    levels, rows = state.shape[1], state.shape[2]
    groups = rows // 8
    lon_even = lax.axis_index("lon") % 2 == 0
    zero = jnp.zeros((8, 128), F32)
    deeps = [depth[8 * g + 4:8 * g + 12, :] for g in range(groups)]
    group = lanes() >> 2
    for pair in range(2):
        def body(k, accs):
            level = k.astype(F32)
            spot_e = group == k
            spot_w = group == ((k + 1) & (levels - 1))
            new = []
            for j in range(2):
                for g in range(groups):
                    q = jnp.where(level < deeps[g], state[2 * pair + j, k, 8 * g:8 * g + 8, :], 0.0)
                    turned = pltpu.roll(q, (4 * k + 4) & 127, 1)
                    new.append(jnp.where(spot_e, turned, accs[len(new)]))
                    new.append(jnp.where(spot_w, turned, accs[len(new)]))
            return tuple(new)

        accs = lax.fori_loop(0, levels, body, (zero,) * (4 * groups), unroll=32)
        for j in range(2):
            for g in range(groups):
                at = slice((2 * pair + j) * rows + 8 * g, (2 * pair + j) * rows + 8 * g + 8)
                east, west = accs[2 * (j * groups + g)], accs[2 * (j * groups + g) + 1]
                la[at, :] = jnp.where(lon_even, east, west)
                lb[at, :] = jnp.where(lon_even, west, east)
    east = west = zero
    for g in range(groups):
        turned = pltpu.roll(deeps[g], 4 * g + 4, 1)
        east = jnp.where(group == g, turned, east)
        west = jnp.where(group == g + 1, turned, west)
    la[4 * rows:4 * rows + 8, :] = jnp.where(lon_even, east, west)
    lb[4 * rows:4 * rows + 8, :] = jnp.where(lon_even, west, east)
    for f in range(4):
        for r in range(2):
            cb[2 * f + r:2 * f + r + 1, :] = edge_rows(lb, f, r)[1]


def coriolis_rows(first, total, order=None):
    row = first + (sublanes() if order is None else order)
    row = jnp.where(row >= total, 2 * total - 1 - row, row)
    return 0.2 + 0.8 * ((row.astype(F32) + 0.5) / total)


def sweep(table, parted, levels, jobs, scale, leave=1.0, unroll=8, unroll_back=8, parts=1, ready=None):
    lane = lanes()
    zero = jnp.zeros((8, 128), F32)
    jobs = [job if len(job) == 9 else (*job, 1, job[2]) for job in jobs]
    turns = [cor * (UNIT * time_step * scale / DRIFT) for _, _, _, _, cor, *_ in jobs]
    uppers = [depth - 1.0 for _, _, _, depth, *_ in jobs]

    def forward(k, carry):
        inner, lowest = table[0, k], table[1, k]
        level = k.astype(F32)
        out = []
        for n, (own, other, o, depth, _, _, _, apart, at) in enumerate(jobs):
            halves = carry[6 * n:6 * n + 4]
            sums = carry[6 * n + 4:6 * n + 6]
            weight = jnp.where(level < uppers[n], inner, jnp.where(level < depth, lowest, 0.0))
            q = [own[f, k, o:o + 8, :] for f in range(4)]
            cu = q[2] * (DRIFT / scale)
            cv = q[3] * (DRIFT / scale)
            prov = []
            near = []
            for f in range(4):
                x = other(f, k) if callable(other) else other[f, k, at:at + 8, :]
                e1 = pltpu.roll(jnp.where(lane == 0, x, q[f]), 127, 1)
                e2 = pltpu.roll(jnp.where(lane < 2, x, q[f]), 126, 1)
                w1 = pltpu.roll(jnp.where(lane == 127, x, q[f]), 1, 1)
                w2 = pltpu.roll(jnp.where(lane >= 126, x, q[f]), 2, 1)
                n1 = own[f, k, o + apart:o + apart + 8, :]
                n2 = own[f, k, o + 2 * apart:o + 2 * apart + 8, :]
                s1 = own[f, k, o - apart:o - apart + 8, :]
                s2 = own[f, k, o - 2 * apart:o - 2 * apart + 8, :]
                dx, dy = e1 - w1, n1 - s1
                near.append((dx, dy))
                slope_x = 8.0 * dx - (e2 - w2)
                slope_y = 8.0 * dy - (n2 - s2)
                if f == 2:
                    slope_y = slope_y - turns[n]
                if f == 3:
                    slope_x = slope_x + turns[n]
                value = CENTRE * q[f] + ((e1 + w1) + (n1 + s1))
                prov.append(value - cu * slope_x - cv * slope_y)
            for axis in range(2):
                half = (PRESS * haline) * near[1][axis] - (PRESS * thermal) * near[0][axis]
                press = sums[axis] + half
                prov[2 + axis] = prov[2 + axis] - press
                near.append(press + half)
            for f in range(4):
                part = (prov[f] + halves[f]) * weight
                parted[n, f, k] = part
                out.append(part)
            out += near[4:6]
        return tuple(out)

    lax.fori_loop(0, levels, forward, (zero,) * (6 * len(jobs)), unroll=unroll)

    def backward(step, carry):
        k = levels - 1 - step
        ratio = table[0, k]
        out = []
        for n, (_, _, _, _, _, dst, d, _, _) in enumerate(jobs):
            for f in range(4):
                value = parted[n, f, k] + ratio * carry[4 * n + f]
                dst[f, k, d:d + 8, :] = value * leave if leave != 1.0 else value
                out.append(value)
        return tuple(out)

    carry = (zero,) * (4 * len(jobs))
    size = levels // parts
    for n in range(parts):
        carry = lax.fori_loop(n * size, (n + 1) * size, backward, carry, unroll=min(unroll_back, size))
        if ready is not None:
            ready(n, levels - (n + 1) * size, size)


def side_tile(east, west, group, k):
    return pltpu.roll(jnp.where(group == k, west, east), (124 - 4 * k) & 127, 1)


def inner_kernel(state, depth, ra, rb, main0, side0, side1, main1, side_depth, last, easts, wests, parted, table):
    levels, rows = state.shape[1], state.shape[2]
    groups = rows // 8
    lon_even = lax.axis_index("lon") % 2 == 0
    first_row = lax.axis_index("lat") * rows
    total = rows * lax.axis_size("lat")
    fill_table(table)
    group = lanes() >> 2
    zero = jnp.zeros((8, 128), F32)

    for n in range(ra.shape[0] // 8):
        at = slice(8 * n, 8 * n + 8)
        a, b = ra[at, :], rb[at, :]
        easts[at, :] = jnp.where(lon_even, a, b)
        wests[at, :] = jnp.where(lon_even, b, a)
    side_depth[0:8, :] = zero
    side_depth[rows:rows + 8, :] = zero
    for g in range(groups):
        at = slice(4 * rows, 4 * rows + 8)
        side_depth[8 * g + 4:8 * g + 12, :] = side_tile(easts[at, :], wests[at, :], group, g)

    def fill(k, unused):
        level = k.astype(F32)
        for g in range(groups):
            at = slice(8 * g, 8 * g + 8)
            to = slice(8 * g + 4, 8 * g + 12)
            is_wet = level < depth[to, :]
            for f in range(4):
                main0[f, k, to, :] = jnp.where(is_wet, state[f, k, at, :], 0.0)
                of = slice(f * rows + 8 * g, f * rows + 8 * g + 8)
                side0[f, k, to, :] = side_tile(easts[of, :], wests[of, :], group, k)
        return unused

    lax.fori_loop(0, levels, fill, 0, unroll=32)

    jobs = []
    for w in range(1, groups):
        o = 8 * w + 2
        cor = coriolis_rows(first_row + (8 * w - 2), total)
        jobs.append((main0, side0, o, depth[o:o + 8, :], cor, main1, 8 * w))
        jobs.append((side0, main0, o, side_depth[o:o + 8, :], cor, side1, 8 * w))
    sweep(table, parted, levels, jobs, 1.0, 1.0, 16, 32)
    jobs = []
    for w in range(1, groups - 1):
        cor = coriolis_rows(first_row + 8 * w, total)
        jobs.append((main1, side1, 8 * w + 2, depth[8 * w + 4:8 * w + 12, :], cor, last, 8 * w - 8))
    sweep(table, parted, levels, jobs, GAIN, 1.0 / GAIN**2, 32, 32)


def south_kernel(p, depth, side_depth, main0, side0, main1, side1, last, rim0, edge0, rim1, edge1, parted, table):
    levels = main0.shape[1]
    rows = depth.shape[0] - 8
    first_row = lax.axis_index("lat") * rows
    total = rows * lax.axis_size("lat")
    has_south = lax.axis_index("lat") > 0
    fill_table(table)
    corner = jnp.where(has_south, p[2 * levels + 1], 0.0)
    rim_depth = jnp.where(has_south, p[2 * levels], 0.0)
    depths = jnp.where(sublanes() < 2, pltpu.roll(rim_depth, 6, 0), depth[2:10, :])

    def fill(k, unused):
        corners = pltpu.roll(corner, (124 - 4 * k) & 127, 1)
        for pair in range(2):
            rim = jnp.where(has_south, p[2 * k + pair], 0.0)
            for j in range(2):
                f = 2 * pair + j
                rim0[f, k, 0:4, :] = rim[4 * j:4 * j + 4, :]
                rim0[f, k, 4:12, :] = main0[f, k, 4:12, :]
                edge0[f, k, 0:2, :] = jnp.zeros((2, 128), F32)
                edge0[f, k, 2:4, :] = corners[2 * f:2 * f + 2, :]
                edge0[f, k, 4:12, :] = side0[f, k, 4:12, :]
                rim1[f, k, 8:12, :] = main1[f, k, 8:12, :]
                edge1[f, k, 8:12, :] = side1[f, k, 8:12, :]
        return unused

    lax.fori_loop(0, levels, fill, 0, unroll=32)
    cor = coriolis_rows(first_row - 2, total)
    sweep(table, parted, levels, [
        (rim0, edge0, 2, depths, cor, rim1, 0),
        (edge0, rim0, 2, side_depth[2:10, :], cor, edge1, 0),
    ], 1.0, 1.0, 32, 16)
    cor = coriolis_rows(first_row, total)
    sweep(table, parted, levels, [(rim1, edge1, 2, depth[4:12, :], cor, last, 0)], GAIN, 1.0 / GAIN**2, 32, 32)


def north_kernel(p1, p2, cb, own_cb, depth, side_depth, main0, side0, main1, side1, middle, south, out,
                 pair0, pair1, rim1, edge1, last, depths, parted, table, sems):
    levels, rows = main0.shape[1], out.shape[2]
    done = [
        pltpu.make_async_copy(middle, out.at[:, :, 8:rows - 8, :], sems.at[0]),
        pltpu.make_async_copy(south, out.at[:, :, 0:8, :], sems.at[1]),
    ]
    for copy in done:
        copy.start()
    band = lax.axis_index("lat")
    band_even = band % 2 == 0
    first_row = band * rows
    total = rows * lax.axis_size("lat")
    is_top = band == lax.axis_size("lat") - 1
    fill_table(table)
    mirror = 127 - lanes()
    flip = sublanes() ^ 3

    def folded(tile):
        return jnp.take_along_axis(tile, mirror, axis=1, mode="promise_in_bounds")

    def ghost(index, sign):
        far = p2[index]
        turned = jnp.take_along_axis(folded(far), flip, axis=0, mode="promise_in_bounds") * sign
        return jnp.where(band_even, p1[index], jnp.where(is_top, turned, far))

    lon, count = lax.axis_index("lon"), lax.axis_size("lon")
    lon_even = lon % 2 == 0
    beyond = jnp.where(lon_even, lon + count - 1, lon + 1) % count
    beside = jnp.where(is_top & (lon + beyond == count - 1), own_cb[...], cb[...])
    far = jnp.where(((lanes() & 3) < 2) == (lon_even != is_top), p2[2 * levels + 1], beside)
    turned = jnp.where(sublanes() < 4, folded(far), -folded(far))
    corner = jnp.where(band_even, p1[2 * levels + 1], jnp.where(is_top, turned, far))
    rim_depth = ghost(2 * levels, 1.0)

    def turns(start, count):
        return pl.ds(start, count, stride=2)

    depths[turns(0, 4), :] = side_depth[rows:rows + 4, :]
    depths[turns(1, 2), :] = depth[rows + 2:rows + 4, :]
    depths[turns(5, 2), :] = rim_depth[0:2, :]

    def fill(k, unused):
        corners = pltpu.roll(corner, jnp.where(is_top, 4 * k - 124, 124 - 4 * k) & 127, 1)
        for pair in range(2):
            rim = ghost(2 * k + pair, 1.0 if pair == 0 else -1.0)
            for j in range(2):
                f = 2 * pair + j
                pair0[f, k, turns(0, 6), :] = side0[f, k, rows - 2:rows + 4, :]
                pair0[f, k, turns(1, 4), :] = main0[f, k, rows:rows + 4, :]
                pair0[f, k, turns(9, 4), :] = rim[4 * j:4 * j + 4, :]
                pair0[f, k, turns(12, 2), :] = corners[2 * f:2 * f + 2, :]
        return unused

    lax.fori_loop(0, levels, fill, 0, unroll=32)
    cor = coriolis_rows(first_row + (rows - 4), total, (sublanes() >> 1) + 2 * (sublanes() & 1))
    first_turn = sublanes() & 1 == 0

    def facing(f, k):
        return jnp.where(first_turn, pair0[f, k, 1:9, :], pair0[f, k, 7:15, :])

    sweep(table, parted, levels, [(pair0, facing, 4, depths[...], cor, pair1, 0, 2, 0)], 1.0, 1.0, 32, 32)

    def split(k, unused):
        for f in range(4):
            rim1[f, k, 0:8, :] = main1[f, k, rows - 8:rows, :]
            rim1[f, k, 8:12, :] = pair1[f, k, turns(1, 4), :]
            edge1[f, k, 0:4, :] = side1[f, k, rows - 6:rows - 2, :]
            edge1[f, k, 4:8, :] = pair1[f, k, turns(0, 4), :]
        return unused

    lax.fori_loop(0, levels, split, 0, unroll=16)
    cor = coriolis_rows(first_row + (rows - 8), total)

    def send(n, k, size):
        done.append(pltpu.make_async_copy(
            last.at[:, k:k + size], out.at[:, k:k + size, rows - 8:rows, :], sems.at[2 + n]))
        done[-1].start()

    sweep(table, parted, levels, [(rim1, edge1, 2, depth[rows - 4:rows + 4, :], cor, last, 0, 1, 0)],
          GAIN, 1.0 / GAIN**2, 32, 32, PARTS, send)
    for copy in done:
        copy.wait()


def per_device(state, land_mask, wet_levels):
    fields, levels, rows, cols = state.shape
    lon, lat = lax.axis_index("lon"), lax.axis_index("lat")
    count, bands = lax.axis_size("lon"), lax.axis_size("lat")

    def mate(i):
        return i ^ 1

    def beyond(i):
        return (i + 1) % count if i % 2 else (i - 1) % count

    def swap(x, to):
        pairs = []
        for i in range(count):
            for b in range(bands):
                ti, tb = to(i, b)
                pairs.append((i * bands + b, ti * bands + tb))
        return lax.ppermute(x, ("lon", "lat"), pairs)

    def near(i, b):
        return i, b ^ 1

    def far(i, b):
        if b == bands - 1:
            return count - 1 - i, b
        if b == 0:
            return mate(i), b
        return i, (b + 1 if b % 2 else b - 1)

    def far_beyond(i, b):
        middle = count - 1 - beyond(i) == i
        if b in (0, bands - 1) and middle:
            return i, bands - 1 - b
        return far(beyond(i), b) if b else (beyond(i), b)

    def call(kernel, vmem, **given):
        return pl.pallas_call(kernel, compiler_params=pltpu.CompilerParams(vmem_limit_bytes=vmem * 2**20), **given)

    shape = lambda *dims: jax.ShapeDtypeStruct(dims, F32)
    block = lambda n: shape(fields, levels, n, 128)
    room = lambda n: pltpu.VMEM((fields, levels, n, 128), F32)
    strip = shape(4 * rows + 8, 128)
    top = call(
        functools.partial(limit_kernel, levels), 4, out_shape=shape(8, 128), out_specs=VM, name="limit",
        cost_estimate=pl.CostEstimate(flops=10**10, bytes_accessed=4096, transcendentals=0),
    )()
    depth = jnp.where(land_mask == 1, jnp.minimum(wet_levels.astype(F32), top[0]), 0.0)
    depth = jnp.pad(depth, ((4, 4), (0, 0)))
    la, lb, cb = call(
        columns_kernel, 4, out_shape=(strip, strip, shape(8, 128)), in_specs=[VM] * 2, out_specs=(VM,) * 3,
        name="columns",
    )(state, depth)
    ra = swap(la, lambda i, b: (mate(i), b))
    rb = swap(lb, lambda i, b: (beyond(i), b))
    rcb = swap(cb, far_beyond)
    p2 = call(
        far_kernel, 4, out_shape=shape(2 * levels + 3, 8, 128), in_specs=[VM] * 3, out_specs=VM, name="far",
    )(state, depth, ra)
    rp2 = swap(p2, far)
    p1 = call(
        near_kernel, 4, out_shape=shape(2 * levels + 2, 8, 128), in_specs=[VM] * 4, out_specs=VM, name="near",
    )(state, depth, ra, rb)
    rp1 = swap(p1, near)
    south = rp1
    if bands > 2:
        same = jnp.where((jnp.arange(128) % 4 < 2) == (lon % 2 == 0), rp2[2 * levels + 1], rcb)
        south = jnp.where(lat % 2 == 0, rp2[:2 * levels + 2].at[2 * levels + 1].set(same), rp1)

    window = lambda n: pltpu.VMEM((n, fields, levels, 8, 128), F32)
    room_table = pltpu.SMEM((2, levels), F32)
    main0, side0, side1, main1, side_depth, last = call(
        inner_kernel,
        10,
        out_shape=(block(rows + 8), block(rows + 8), block(rows + 4), block(rows + 4), shape(rows + 8, 128),
                   block(rows - 16)),
        in_specs=[VM] * 4,
        out_specs=(VM,) * 6,
        scratch_shapes=[pltpu.VMEM((4 * rows + 8, 128), F32), pltpu.VMEM((4 * rows + 8, 128), F32),
                        window(rows // 4 - 2), room_table],
        name="inner",
    )(state, depth, ra, rb)
    first = call(
        south_kernel,
        10,
        out_shape=block(8),
        in_specs=[VM] * 7,
        out_specs=VM,
        scratch_shapes=[room(16)] * 4 + [window(2), room_table],
        name="south",
    )(south, depth, side_depth, main0, side0, main1, side1)
    return call(
        north_kernel,
        12,
        out_shape=shape(*state.shape),
        in_specs=[VM] * 12,
        out_specs=HB,
        scratch_shapes=[room(16), room(8), room(16), room(8), room(8), pltpu.VMEM((8, 128), F32), window(1), room_table,
                        pltpu.SemaphoreType.DMA((2 + PARTS,))],
        name="north",
    )(rp1, rp2, rcb, cb, depth, side_depth, main0, side0, main1, side1, last, first)


def solution(mesh):
    placed = (P(None, None, "lat", "lon"), P("lat", "lon"), P("lat", "lon"))
    return jax.shard_map(
        per_device,
        mesh=mesh,
        in_specs=placed,
        out_specs=P(None, None, "lat", "lon"),
        check_vma=False,
    )
```

```python
import functools

import jax
import jax.numpy as jnp
import numpy as np
from jax import lax
from jax.experimental import pallas as pl
from jax.experimental.pallas import tpu as pltpu
from jax.sharding import PartitionSpec as P

STEPS = 2
time_step = 0.1
lateral_mix = 0.5
column_mix = 0.5
gravity = 0.5
thermal = 0.2
haline = 0.8

F32 = jnp.float32
PARTS = 4
VM = pl.BlockSpec(memory_space=pltpu.VMEM)
HB = pl.BlockSpec(memory_space=pltpu.HBM)


UNIT = 1.0 / (time_step * lateral_mix)
GAIN = column_mix * UNIT
CENTRE = UNIT * (1.0 - 4.0 * time_step * lateral_mix)
DRIFT = UNIT * time_step / 12.0
PRESS = UNIT * time_step * 0.5 * gravity * 0.5


def factors(levels):
    inner = np.zeros(levels)
    lowest = np.zeros(levels)
    for k in range(levels):
        over = column_mix if k > 0 else 0.0
        less = column_mix * inner[k - 1] if k > 0 else 0.0
        inner[k] = column_mix / (1.0 + over + column_mix - less)
        lowest[k] = column_mix / (1.0 + over - less)
    return np.stack([inner, lowest]).astype(np.float32)


def fill_table(table):
    for n, row in enumerate(factors(table.shape[1])):
        for k, value in enumerate(row):
            table[n, k] = float(value)


def over(start, stop, body, carry, unroll):
    if unroll < stop - start:
        return lax.fori_loop(start, stop, body, carry, unroll=unroll)
    for k in range(start, stop):
        carry = body(k, carry)
    return carry


def lanes():
    return lax.broadcasted_iota(jnp.int32, (8, 128), 1)


def sublanes():
    return lax.broadcasted_iota(jnp.int32, (8, 128), 0)


def limit_kernel(levels, top):
    top[...] = jnp.full(top.shape, float(levels), F32)


def edge_rows(strip, f, r):
    rows = (strip.shape[0] - 8) // 4
    base = f * rows
    band = lax.axis_index("lat")
    band_even = band % 2 == 0
    is_top = band == lax.axis_size("lat") - 1
    south, north = strip[base + r:base + r + 1, :], strip[base + rows - 2 + r:base + rows - 1 + r, :]
    folded = strip[base + rows - 1 - r:base + rows - r, :]
    return jnp.where(band_even, north, south), jnp.where(band_even, south, jnp.where(is_top, folded, north))


def row_tiles(state, k, deep_s, deep_n, pair):
    rows = state.shape[2]
    level = k.astype(F32)
    tiles = []
    for f in (2 * pair, 2 * pair + 1):
        tiles.append(jnp.where(level < deep_s, state[f, k, 0:8, :], 0.0))
        tiles.append(jnp.where(level < deep_n, state[f, k, rows - 8:rows, :], 0.0))
    return join_rows(*tiles)


def join_rows(a_s, a_n, b_s, b_n):
    band_even = lax.axis_index("lat") % 2 == 0
    low = sublanes() < 4
    north = jnp.where(low, pltpu.roll(a_n, 4, 0), b_n)
    south = jnp.where(low, a_s, pltpu.roll(b_s, 4, 0))
    return jnp.where(band_even, north, south), jnp.where(band_even, south, north)


def far_kernel(state, depth, ra, p2):
    levels, rows = state.shape[1], state.shape[2]
    deep_s, deep_n = depth[4:12, :], depth[rows - 4:rows + 4, :]

    def body(k, unused):
        for pair in range(2):
            p2[2 * k + pair] = row_tiles(state, k, deep_s, deep_n, pair)[1]
        return unused

    lax.fori_loop(0, levels, body, 0, unroll=8)
    p2[2 * levels] = join_rows(deep_s, deep_n, deep_s, deep_n)[1]
    for f in range(4):
        for r in range(2):
            p2[2 * levels + 1, 2 * f + r:2 * f + r + 1, :] = edge_rows(ra, f, r)[1]
    for n in range(2 * levels + 2, p2.shape[0]):
        p2[n] = jnp.zeros((8, 128), F32)


def near_kernel(state, depth, ra, rb, p1):
    levels, rows = state.shape[1], state.shape[2]
    deep_s, deep_n = depth[4:12, :], depth[rows - 4:rows + 4, :]
    from_a = ((lanes()[0:1] & 3) < 2) == (lax.axis_index("lon") % 2 == 0)

    def body(k, unused):
        for pair in range(2):
            p1[2 * k + pair] = row_tiles(state, k, deep_s, deep_n, pair)[0]
        return unused

    lax.fori_loop(0, levels, body, 0, unroll=8)
    p1[2 * levels] = join_rows(deep_s, deep_n, deep_s, deep_n)[0]
    for f in range(4):
        for r in range(2):
            row = jnp.where(from_a, edge_rows(ra, f, r)[0], edge_rows(rb, f, r)[0])
            p1[2 * levels + 1, 2 * f + r:2 * f + r + 1, :] = row


def columns_kernel(state, depth, la, lb, cb):
    levels, rows = state.shape[1], state.shape[2]
    groups = rows // 8
    lon_even = lax.axis_index("lon") % 2 == 0
    zero = jnp.zeros((8, 128), F32)
    deeps = [depth[8 * g + 4:8 * g + 12, :] for g in range(groups)]
    group = lanes() >> 2
    for pair in range(2):
        def body(k, accs):
            level = k.astype(F32)
            spot_e = group == k
            spot_w = group == ((k + 1) & (levels - 1))
            new = []
            for j in range(2):
                for g in range(groups):
                    q = jnp.where(level < deeps[g], state[2 * pair + j, k, 8 * g:8 * g + 8, :], 0.0)
                    turned = pltpu.roll(q, (4 * k + 4) & 127, 1)
                    new.append(jnp.where(spot_e, turned, accs[len(new)]))
                    new.append(jnp.where(spot_w, turned, accs[len(new)]))
            return tuple(new)

        accs = lax.fori_loop(0, levels, body, (zero,) * (4 * groups), unroll=32)
        for j in range(2):
            for g in range(groups):
                at = slice((2 * pair + j) * rows + 8 * g, (2 * pair + j) * rows + 8 * g + 8)
                east, west = accs[2 * (j * groups + g)], accs[2 * (j * groups + g) + 1]
                la[at, :] = jnp.where(lon_even, east, west)
                lb[at, :] = jnp.where(lon_even, west, east)
    east = west = zero
    for g in range(groups):
        turned = pltpu.roll(deeps[g], 4 * g + 4, 1)
        east = jnp.where(group == g, turned, east)
        west = jnp.where(group == g + 1, turned, west)
    la[4 * rows:4 * rows + 8, :] = jnp.where(lon_even, east, west)
    lb[4 * rows:4 * rows + 8, :] = jnp.where(lon_even, west, east)
    for f in range(4):
        for r in range(2):
            cb[2 * f + r:2 * f + r + 1, :] = edge_rows(lb, f, r)[1]


def coriolis_rows(first, total, order=None):
    row = first + (sublanes() if order is None else order)
    row = jnp.where(row >= total, 2 * total - 1 - row, row)
    return 0.2 + 0.8 * ((row.astype(F32) + 0.5) / total)


def sweep(table, parted, levels, jobs, scale, leave=1.0, unroll=8, unroll_back=8, parts=1, ready=None):
    lane = lanes()
    zero = jnp.zeros((8, 128), F32)
    jobs = [job if len(job) == 9 else (*job, 1, job[2]) for job in jobs]
    fixed = factors(levels)
    turns = [cor * (UNIT * time_step * scale / DRIFT) for _, _, _, _, cor, *_ in jobs]
    uppers = [depth - 1.0 for _, _, _, depth, *_ in jobs]

    def forward(k, carry):
        if isinstance(k, int):
            inner, lowest, level = float(fixed[0, k]), float(fixed[1, k]), float(k)
        else:
            inner, lowest, level = table[0, k], table[1, k], k.astype(F32)
        out = []
        for n, (own, other, o, depth, _, _, _, apart, at) in enumerate(jobs):
            halves = carry[6 * n:6 * n + 4]
            sums = carry[6 * n + 4:6 * n + 6]
            weight = jnp.where(level < uppers[n], inner, jnp.where(level < depth, lowest, 0.0))
            q = [own[f, k, o:o + 8, :] for f in range(4)]
            cu = q[2] * (DRIFT / scale)
            cv = q[3] * (DRIFT / scale)
            prov = []
            near = []
            for f in range(4):
                x = other(f, k) if callable(other) else other[f, k, at:at + 8, :]
                e1 = pltpu.roll(jnp.where(lane == 0, x, q[f]), 127, 1)
                e2 = pltpu.roll(jnp.where(lane < 2, x, q[f]), 126, 1)
                w1 = pltpu.roll(jnp.where(lane == 127, x, q[f]), 1, 1)
                w2 = pltpu.roll(jnp.where(lane >= 126, x, q[f]), 2, 1)
                n1 = own[f, k, o + apart:o + apart + 8, :]
                n2 = own[f, k, o + 2 * apart:o + 2 * apart + 8, :]
                s1 = own[f, k, o - apart:o - apart + 8, :]
                s2 = own[f, k, o - 2 * apart:o - 2 * apart + 8, :]
                dx, dy = e1 - w1, n1 - s1
                near.append((dx, dy))
                slope_x = 8.0 * dx - (e2 - w2)
                slope_y = 8.0 * dy - (n2 - s2)
                if f == 2:
                    slope_y = slope_y - turns[n]
                if f == 3:
                    slope_x = slope_x + turns[n]
                value = CENTRE * q[f] + ((e1 + w1) + (n1 + s1))
                prov.append(value - cu * slope_x - cv * slope_y)
            for axis in range(2):
                half = (PRESS * haline) * near[1][axis] - (PRESS * thermal) * near[0][axis]
                press = sums[axis] + half
                prov[2 + axis] = prov[2 + axis] - press
                near.append(press + half)
            for f in range(4):
                part = (prov[f] + halves[f]) * weight
                parted[n, f, k] = part
                out.append(part)
            out += near[4:6]
        return tuple(out)

    over(0, levels, forward, (zero,) * (6 * len(jobs)), unroll)

    def backward(step, carry):
        k = levels - 1 - step
        ratio = float(fixed[0, k]) if isinstance(k, int) else table[0, k]
        out = []
        for n, (_, _, _, _, _, dst, d, _, _) in enumerate(jobs):
            for f in range(4):
                value = parted[n, f, k] + ratio * carry[4 * n + f]
                dst[f, k, d:d + 8, :] = value * leave if leave != 1.0 else value
                out.append(value)
        return tuple(out)

    carry = (zero,) * (4 * len(jobs))
    size = levels // parts
    for n in range(parts):
        carry = over(n * size, (n + 1) * size, backward, carry, min(unroll_back, size))
        if ready is not None:
            ready(n, levels - (n + 1) * size, size)


def side_tile(east, west, group, k):
    return pltpu.roll(jnp.where(group == k, west, east), (124 - 4 * k) & 127, 1)


def inner_kernel(state, depth, ra, rb, main0, side0, side1, main1, side_depth, last, easts, wests, parted, table):
    levels, rows = state.shape[1], state.shape[2]
    groups = rows // 8
    lon_even = lax.axis_index("lon") % 2 == 0
    first_row = lax.axis_index("lat") * rows
    total = rows * lax.axis_size("lat")
    fill_table(table)
    group = lanes() >> 2
    zero = jnp.zeros((8, 128), F32)

    for n in range(ra.shape[0] // 8):
        at = slice(8 * n, 8 * n + 8)
        a, b = ra[at, :], rb[at, :]
        easts[at, :] = jnp.where(lon_even, a, b)
        wests[at, :] = jnp.where(lon_even, b, a)
    side_depth[0:8, :] = zero
    side_depth[rows:rows + 8, :] = zero
    for g in range(groups):
        at = slice(4 * rows, 4 * rows + 8)
        side_depth[8 * g + 4:8 * g + 12, :] = side_tile(easts[at, :], wests[at, :], group, g)

    def fill(k, unused):
        level = k.astype(F32)
        for g in range(groups):
            at = slice(8 * g, 8 * g + 8)
            to = slice(8 * g + 4, 8 * g + 12)
            is_wet = level < depth[to, :]
            for f in range(4):
                main0[f, k, to, :] = jnp.where(is_wet, state[f, k, at, :], 0.0)
                of = slice(f * rows + 8 * g, f * rows + 8 * g + 8)
                side0[f, k, to, :] = side_tile(easts[of, :], wests[of, :], group, k)
        return unused

    lax.fori_loop(0, levels, fill, 0, unroll=32)

    jobs = []
    for w in range(1, groups):
        o = 8 * w + 2
        cor = coriolis_rows(first_row + (8 * w - 2), total)
        jobs.append((main0, side0, o, depth[o:o + 8, :], cor, main1, 8 * w))
        jobs.append((side0, main0, o, side_depth[o:o + 8, :], cor, side1, 8 * w))
    sweep(table, parted, levels, jobs, 1.0, 1.0, 16, 32)
    jobs = []
    for w in range(1, groups - 1):
        cor = coriolis_rows(first_row + 8 * w, total)
        jobs.append((main1, side1, 8 * w + 2, depth[8 * w + 4:8 * w + 12, :], cor, last, 8 * w - 8))
    sweep(table, parted, levels, jobs, GAIN, 1.0 / GAIN**2, 32, 32)


def south_kernel(p, depth, side_depth, main0, side0, main1, side1, last, rim0, edge0, rim1, edge1, parted, table):
    levels = main0.shape[1]
    rows = depth.shape[0] - 8
    first_row = lax.axis_index("lat") * rows
    total = rows * lax.axis_size("lat")
    has_south = lax.axis_index("lat") > 0
    corner = jnp.where(has_south, p[2 * levels + 1], 0.0)
    rim_depth = jnp.where(has_south, p[2 * levels], 0.0)
    depths = jnp.where(sublanes() < 2, pltpu.roll(rim_depth, 6, 0), depth[2:10, :])

    def fill(k, unused):
        corners = pltpu.roll(corner, (124 - 4 * k) & 127, 1)
        for pair in range(2):
            rim = jnp.where(has_south, p[2 * k + pair], 0.0)
            for j in range(2):
                f = 2 * pair + j
                rim0[f, k, 0:4, :] = rim[4 * j:4 * j + 4, :]
                rim0[f, k, 4:12, :] = main0[f, k, 4:12, :]
                edge0[f, k, 0:2, :] = jnp.zeros((2, 128), F32)
                edge0[f, k, 2:4, :] = corners[2 * f:2 * f + 2, :]
                edge0[f, k, 4:12, :] = side0[f, k, 4:12, :]
                rim1[f, k, 8:12, :] = main1[f, k, 8:12, :]
                edge1[f, k, 8:12, :] = side1[f, k, 8:12, :]
        return unused

    lax.fori_loop(0, levels, fill, 0, unroll=32)
    cor = coriolis_rows(first_row - 2, total)
    sweep(table, parted, levels, [
        (rim0, edge0, 2, depths, cor, rim1, 0),
        (edge0, rim0, 2, side_depth[2:10, :], cor, edge1, 0),
    ], 1.0, 1.0, 32, 16)
    cor = coriolis_rows(first_row, total)
    sweep(table, parted, levels, [(rim1, edge1, 2, depth[4:12, :], cor, last, 0)], GAIN, 1.0 / GAIN**2, 32, 32)


def north_kernel(p1, p2, cb, own_cb, depth, side_depth, main0, side0, main1, side1, middle, south, out,
                 pair0, pair1, rim1, edge1, last, depths, parted, table, sems):
    levels, rows = main0.shape[1], out.shape[2]
    done = [
        pltpu.make_async_copy(middle, out.at[:, :, 8:rows - 8, :], sems.at[0]),
        pltpu.make_async_copy(south, out.at[:, :, 0:8, :], sems.at[1]),
    ]
    for copy in done:
        copy.start()
    band = lax.axis_index("lat")
    band_even = band % 2 == 0
    first_row = band * rows
    total = rows * lax.axis_size("lat")
    is_top = band == lax.axis_size("lat") - 1
    mirror = 127 - lanes()
    flip = sublanes() ^ 3

    def folded(tile):
        return jnp.take_along_axis(tile, mirror, axis=1, mode="promise_in_bounds")

    def ghost(index, sign):
        far = p2[index]
        turned = jnp.take_along_axis(folded(far), flip, axis=0, mode="promise_in_bounds") * sign
        return jnp.where(band_even, p1[index], jnp.where(is_top, turned, far))

    lon, count = lax.axis_index("lon"), lax.axis_size("lon")
    lon_even = lon % 2 == 0
    beyond = jnp.where(lon_even, lon + count - 1, lon + 1) % count
    beside = jnp.where(is_top & (lon + beyond == count - 1), own_cb[...], cb[...])
    far = jnp.where(((lanes() & 3) < 2) == (lon_even != is_top), p2[2 * levels + 1], beside)
    turned = jnp.where(sublanes() < 4, folded(far), -folded(far))
    corner = jnp.where(band_even, p1[2 * levels + 1], jnp.where(is_top, turned, far))
    rim_depth = ghost(2 * levels, 1.0)

    def turns(start, count):
        return pl.ds(start, count, stride=2)

    depths[turns(0, 4), :] = side_depth[rows:rows + 4, :]
    depths[turns(1, 2), :] = depth[rows + 2:rows + 4, :]
    depths[turns(5, 2), :] = rim_depth[0:2, :]

    def fill(k, unused):
        corners = pltpu.roll(corner, jnp.where(is_top, 4 * k - 124, 124 - 4 * k) & 127, 1)
        for pair in range(2):
            rim = ghost(2 * k + pair, 1.0 if pair == 0 else -1.0)
            for j in range(2):
                f = 2 * pair + j
                pair0[f, k, turns(0, 6), :] = side0[f, k, rows - 2:rows + 4, :]
                pair0[f, k, turns(1, 4), :] = main0[f, k, rows:rows + 4, :]
                pair0[f, k, turns(9, 4), :] = rim[4 * j:4 * j + 4, :]
                pair0[f, k, turns(12, 2), :] = corners[2 * f:2 * f + 2, :]
        return unused

    lax.fori_loop(0, levels, fill, 0, unroll=32)
    cor = coriolis_rows(first_row + (rows - 4), total, (sublanes() >> 1) + 2 * (sublanes() & 1))
    first_turn = sublanes() & 1 == 0

    def facing(f, k):
        return jnp.where(first_turn, pair0[f, k, 1:9, :], pair0[f, k, 7:15, :])

    sweep(table, parted, levels, [(pair0, facing, 4, depths[...], cor, pair1, 0, 2, 0)], 1.0, 1.0, 32, 32)

    def split(k, unused):
        for f in range(4):
            rim1[f, k, 0:8, :] = main1[f, k, rows - 8:rows, :]
            rim1[f, k, 8:12, :] = pair1[f, k, turns(1, 4), :]
            edge1[f, k, 0:4, :] = side1[f, k, rows - 6:rows - 2, :]
            edge1[f, k, 4:8, :] = pair1[f, k, turns(0, 4), :]
        return unused

    lax.fori_loop(0, levels, split, 0, unroll=16)
    cor = coriolis_rows(first_row + (rows - 8), total)

    def send(n, k, size):
        done.append(pltpu.make_async_copy(
            last.at[:, k:k + size], out.at[:, k:k + size, rows - 8:rows, :], sems.at[2 + n]))
        done[-1].start()

    sweep(table, parted, levels, [(rim1, edge1, 2, depth[rows - 4:rows + 4, :], cor, last, 0, 1, 0)],
          GAIN, 1.0 / GAIN**2, 32, 32, PARTS, send)
    for copy in done:
        copy.wait()


def per_device(state, land_mask, wet_levels):
    fields, levels, rows, cols = state.shape
    lon, lat = lax.axis_index("lon"), lax.axis_index("lat")
    count, bands = lax.axis_size("lon"), lax.axis_size("lat")

    def mate(i):
        return i ^ 1

    def beyond(i):
        return (i + 1) % count if i % 2 else (i - 1) % count

    def swap(x, to):
        pairs = []
        for i in range(count):
            for b in range(bands):
                ti, tb = to(i, b)
                pairs.append((i * bands + b, ti * bands + tb))
        return lax.ppermute(x, ("lon", "lat"), pairs)

    def near(i, b):
        return i, b ^ 1

    def far(i, b):
        if b == bands - 1:
            return count - 1 - i, b
        if b == 0:
            return mate(i), b
        return i, (b + 1 if b % 2 else b - 1)

    def far_beyond(i, b):
        middle = count - 1 - beyond(i) == i
        if b in (0, bands - 1) and middle:
            return i, bands - 1 - b
        return far(beyond(i), b) if b else (beyond(i), b)

    def call(kernel, vmem, **given):
        return pl.pallas_call(kernel, compiler_params=pltpu.CompilerParams(vmem_limit_bytes=vmem * 2**20), **given)

    shape = lambda *dims: jax.ShapeDtypeStruct(dims, F32)
    block = lambda n: shape(fields, levels, n, 128)
    room = lambda n: pltpu.VMEM((fields, levels, n, 128), F32)
    strip = shape(4 * rows + 8, 128)
    top = call(
        functools.partial(limit_kernel, levels), 4, out_shape=shape(8, 128), out_specs=VM, name="limit",
        cost_estimate=pl.CostEstimate(flops=10**10, bytes_accessed=4096, transcendentals=0),
    )()
    depth = jnp.where(land_mask == 1, jnp.minimum(wet_levels.astype(F32), top[0]), 0.0)
    depth = jnp.pad(depth, ((4, 4), (0, 0)))
    la, lb, cb = call(
        columns_kernel, 4, out_shape=(strip, strip, shape(8, 128)), in_specs=[VM] * 2, out_specs=(VM,) * 3,
        name="columns",
    )(state, depth)
    ra = swap(la, lambda i, b: (mate(i), b))
    rb = swap(lb, lambda i, b: (beyond(i), b))
    rcb = swap(cb, far_beyond)
    p2 = call(
        far_kernel, 4, out_shape=shape(2 * levels + 3, 8, 128), in_specs=[VM] * 3, out_specs=VM, name="far",
    )(state, depth, ra)
    rp2 = swap(p2, far)
    p1 = call(
        near_kernel, 4, out_shape=shape(2 * levels + 2, 8, 128), in_specs=[VM] * 4, out_specs=VM, name="near",
    )(state, depth, ra, rb)
    rp1 = swap(p1, near)
    south = rp1
    if bands > 2:
        same = jnp.where((jnp.arange(128) % 4 < 2) == (lon % 2 == 0), rp2[2 * levels + 1], rcb)
        south = jnp.where(lat % 2 == 0, rp2[:2 * levels + 2].at[2 * levels + 1].set(same), rp1)

    window = lambda n: pltpu.VMEM((n, fields, levels, 8, 128), F32)
    room_table = pltpu.SMEM((2, levels), F32)
    main0, side0, side1, main1, side_depth, last = call(
        inner_kernel,
        10,
        out_shape=(block(rows + 8), block(rows + 8), block(rows + 4), block(rows + 4), shape(rows + 8, 128),
                   block(rows - 16)),
        in_specs=[VM] * 4,
        out_specs=(VM,) * 6,
        scratch_shapes=[pltpu.VMEM((4 * rows + 8, 128), F32), pltpu.VMEM((4 * rows + 8, 128), F32),
                        window(rows // 4 - 2), room_table],
        name="inner",
    )(state, depth, ra, rb)
    first = call(
        south_kernel,
        10,
        out_shape=block(8),
        in_specs=[VM] * 7,
        out_specs=VM,
        scratch_shapes=[room(16)] * 4 + [window(2), room_table],
        name="south",
    )(south, depth, side_depth, main0, side0, main1, side1)
    return call(
        north_kernel,
        12,
        out_shape=shape(*state.shape),
        in_specs=[VM] * 12,
        out_specs=HB,
        scratch_shapes=[room(16), room(8), room(16), room(8), room(8), pltpu.VMEM((8, 128), F32), window(1), room_table,
                        pltpu.SemaphoreType.DMA((2 + PARTS,))],
        name="north",
    )(rp1, rp2, rcb, cb, depth, side_depth, main0, side0, main1, side1, last, first)


def solution(mesh):
    placed = (P(None, None, "lat", "lon"), P("lat", "lon"), P("lat", "lon"))
    return jax.shard_map(
        per_device,
        mesh=mesh,
        in_specs=placed,
        out_specs=P(None, None, "lat", "lon"),
        check_vma=False,
    )
```
